32 devices in a mesh: lon: 8 (over y, x, core), lat: 4 (over z).
Axes of the slice: x: 2, y: 2, z: 4, core: 2. Of those that a mesh axis runs over, the one named last changes fastest.
Arguments:
- tokens: bfloat16 [1, 2, 168, 96, 512], P(None, None, 'lat', 'lon'), may hold values from -200 to 200
- group_ids: int32 [168, 96], replicated, may hold values from 0 to 1
- bias_table: float32 [759, 16], replicated, may hold values from -4 to 4
- w_qkv: bfloat16 [512, 1536], replicated, may hold values from -0.25 to 0.25
- w_proj: bfloat16 [512, 512], replicated, may hold values from -0.25 to 0.25
- gain_attn: float32 [512], replicated, may hold values from 0.5 to 1.5
- w_in: bfloat16 [512, 2048], replicated, may hold values from -0.25 to 0.25
- w_out: bfloat16 [2048, 512], replicated, may hold values from -0.125 to 0.125
- gain_mlp: float32 [512], replicated, may hold values from 0.5 to 1.5
Outputs:
- result: bfloat16 [1, 2, 168, 96, 512], P(None, None, 'lat', 'lon')
The draws below stay inside these ranges and needn't reach their ends.
All inputs are finite; a program needn't handle non-finite values.
Results may differ from the reference program's by a relative error of at most 0.0085.
Values may be sent and summed in bfloat16 or wider, within the bound.
No kernel may reach another device: no remote copies, remote signals or barrier semaphores. Data moves between devices by JAX's collectives and lax.ppermute only.
A program may use at most 128 MiB of HBM per device.

```python
import jax
import jax.numpy as jnp
from jax import lax

D = 512
HEADS = 16
FF = 2048
WIN_LEV = 2
WIN_LAT = 6
WIN_LON = 12
SHIFT_LAT = 3
SHIFT_LON = 6
LEVELS = 2
SAMPLES = 1
LAT = 168
LON = 96
NUM_REL = 759


def draw_tokens(key, part):
    key = jax.random.fold_in(key, 11)
    first = jax.random.fold_in(key, 0)
    shape = (SAMPLES, LEVELS, LAT, LON, D)
    base = jnp.clip(jax.random.normal(first, shape, jnp.float32), -4.0, 4.0)
    return base.astype(jnp.bfloat16)


def touch_ends(array, rng, low, largest):
    dims = array.shape
    spot = [jax.random.randint(jax.random.fold_in(rng, axis), (), 0, dims[axis]) for axis in range(len(dims))]
    array = array.at[tuple(spot)].set(low)
    longest = dims.index(max(dims))
    spot[longest] = (spot[longest] + 1) % dims[longest]
    return array.at[tuple(spot)].set(largest)


def gaussian(stream_key, dims, scale, reach, held_as=jnp.bfloat16):
    return jnp.clip(scale * jax.random.normal(stream_key, dims, jnp.float32), -reach, reach).astype(held_as)


def setup_inputs(seed: int = 0) -> dict:
    arg_keys = jax.random.split(jax.random.key(seed), 10)
    tokens = draw_tokens(jax.random.fold_in(arg_keys[9], 71), 0)
    group_ids = touch_ends(jax.random.randint(arg_keys[1], (LAT, LON), 0, 2), jax.random.fold_in(arg_keys[1], 1), 0, 1).astype(jnp.int32)
    bias_table = gaussian(arg_keys[2], (NUM_REL, HEADS), 1.0, 4.0, jnp.float32)
    w_qkv = gaussian(arg_keys[3], (D, 3 * D), D ** -0.5, 0.25)
    w_proj = gaussian(arg_keys[4], (D, D), D ** -0.5, 0.25)
    gain_attn = jnp.clip(1.0 + 0.1 * jax.random.normal(arg_keys[5], (D,), jnp.float32), 0.5, 1.5)
    w_in = gaussian(arg_keys[6], (D, FF), D ** -0.5, 0.25)
    w_out = gaussian(arg_keys[7], (FF, D), FF ** -0.5, 0.125)
    gain_mlp = jnp.clip(1.0 + 0.1 * jax.random.normal(arg_keys[8], (D,), jnp.float32), 0.5, 1.5)
    return dict(tokens=tokens, group_ids=group_ids, bias_table=bias_table, w_qkv=w_qkv, w_proj=w_proj, gain_attn=gain_attn, w_in=w_in, w_out=w_out, gain_mlp=gain_mlp)


EPS = 1e-05

def layer_norm(value, gain):
    mean = lax.optimization_barrier(jnp.mean(value, -1, keepdims=True))
    centred = value - mean
    var = lax.optimization_barrier(jnp.mean(centred * centred, -1, keepdims=True))
    return centred * lax.rsqrt(var + EPS) * gain

def relative_bias(bias_table):
    count = WIN_LEV * WIN_LAT * WIN_LON
    place = jnp.arange(count, dtype=jnp.int32)
    zpos = place // (WIN_LAT * WIN_LON)
    hpos = place // WIN_LON % WIN_LAT
    wpos = place % WIN_LON
    rel = (zpos[:, None] - zpos[None, :] + WIN_LEV - 1) * ((2 * WIN_LAT - 1) * (2 * WIN_LON - 1))
    rel = rel + (hpos[:, None] - hpos[None, :] + WIN_LAT - 1) * (2 * WIN_LON - 1)
    rel = rel + (wpos[:, None] - wpos[None, :] + WIN_LON - 1)
    return jnp.transpose(bias_table[rel], (2, 0, 1))

def partition(value):
    b, z, h, w, c = value.shape
    value = value.reshape(b, z // WIN_LEV, WIN_LEV, h // WIN_LAT, WIN_LAT, w // WIN_LON, WIN_LON, c)
    value = jnp.transpose(value, (0, 1, 3, 5, 2, 4, 6, 7))
    return value.reshape(-1, WIN_LEV * WIN_LAT * WIN_LON, c)

def unpartition(value, shape):
    b, z, h, w, c = shape
    value = value.reshape(b, z // WIN_LEV, h // WIN_LAT, w // WIN_LON, WIN_LEV, WIN_LAT, WIN_LON, c)
    value = jnp.transpose(value, (0, 1, 4, 2, 5, 3, 6, 7))
    return value.reshape(b, z, h, w, c)

def attend(shifted, label, bias, w_qkv, w_proj, gain_attn):
    b, z, h, w, c = shifted.shape
    windows = partition(shifted)
    labels = partition(jnp.broadcast_to(label[None, None, :, :, None], (b, z, h, w, 1)))[:, :, 0]
    heads = bias.shape[0]
    head_dim = c // heads
    scale = 1.0 / head_dim ** 0.5

    def one_window(pair):
        window, marks = pair
        count = window.shape[0]
        qkv = jnp.dot(window, w_qkv, preferred_element_type=jnp.float32).astype(jnp.bfloat16)
        qkv = qkv.reshape(count, 3, heads, head_dim)
        query = qkv[:, 0].astype(jnp.float32)
        keys = qkv[:, 1].astype(jnp.float32)
        values = qkv[:, 2].astype(jnp.float32)
        scores = jnp.einsum('thd,shd->hts', query, keys) * scale + bias
        allowed = marks[:, None] == marks[None, :]
        scores = jnp.where(allowed[None], scores, -jnp.inf)
        top = lax.optimization_barrier(jnp.max(scores, -1, keepdims=True))
        expo = jnp.exp(scores - top)
        weights = (expo / lax.optimization_barrier(jnp.sum(expo, -1, keepdims=True))).astype(jnp.bfloat16)
        heads_out = jnp.einsum('hts,shd->thd', weights.astype(jnp.float32), values)
        heads_out = heads_out.reshape(count, c).astype(jnp.bfloat16)
        proj = jnp.dot(heads_out, w_proj, preferred_element_type=jnp.float32)
        return layer_norm(proj, gain_attn).astype(jnp.bfloat16)
    out = lax.map(one_window, (windows, labels))
    return unpartition(out, shifted.shape)

def reference(tokens, group_ids, bias_table, w_qkv, w_proj, gain_attn, w_in, w_out, gain_mlp):
    shifted = jnp.roll(tokens, (-SHIFT_LAT, -SHIFT_LON), axis=(2, 3))
    region = (jnp.arange(LAT) >= LAT - SHIFT_LAT).astype(jnp.int32)
    label = group_ids * 2 + region[:, None]
    bias = relative_bias(bias_table)
    branch = attend(shifted, label, bias, w_qkv, w_proj, gain_attn)
    branch = jnp.roll(branch, (SHIFT_LAT, SHIFT_LON), axis=(2, 3))
    mid = (tokens.astype(jnp.float32) + branch.astype(jnp.float32)).astype(jnp.bfloat16)
    lines = mid.reshape(-1, LON, D)

    def one_line(line):
        hidden = jax.nn.gelu(jnp.dot(line, w_in, preferred_element_type=jnp.float32), approximate=False)
        hidden = hidden.astype(jnp.bfloat16)
        down = jnp.dot(hidden, w_out, preferred_element_type=jnp.float32)
        return (line.astype(jnp.float32) + layer_norm(down, gain_mlp)).astype(jnp.bfloat16)
    result = lax.map(one_line, lines)
    return result.reshape(tokens.shape)
```

```python
import functools

import jax
import jax.numpy as jnp
from jax import lax
from jax.experimental import pallas as pl
from jax.experimental.pallas import tpu as pltpu
from jax.sharding import PartitionSpec as P

WIN_LEV = 2
WIN_LAT = 6
WIN_LON = 12
SHIFT_LAT = 3
SHIFT_LON = 6

EPS = 1e-05
LOG2E = 1.4426950408889634
HALF = WIN_LEV * WIN_LAT * SHIFT_LON
ROW = WIN_LEV * SHIFT_LON
EDGE = SHIFT_LAT * ROW
KEYS = 2 * HALF
LANES = 256
GROUP = 4
VMEM_LIMIT = 50 * 1024 * 1024

F32 = jnp.float32
BF16 = jnp.bfloat16


def params():
    return pltpu.CompilerParams(vmem_limit_bytes=VMEM_LIMIT)


def vmem(count):
    return [pl.BlockSpec(memory_space=pltpu.VMEM)] * count


def pack_kernel(par_ref, tok_ref, near_ref, far_ref, top_ref, bot_ref, scr):
    lev, lat = tok_ref.shape[0], tok_ref.shape[1]
    par = par_ref[0]
    for h in range(lat):
        for z in range(lev):
            x = tok_ref[z, h].astype(F32)
            off = h * ROW + z * SHIFT_LON
            scr[1 - par, off : off + SHIFT_LON, :] = x[:SHIFT_LON]
            scr[par, off : off + SHIFT_LON, :] = x[SHIFT_LON:]
    rows = lat * ROW
    near_ref[...] = scr[0, EDGE : rows - EDGE, :].astype(BF16)
    far_ref[...] = scr[1, EDGE : rows - EDGE, :].astype(BF16)
    for side in range(2):
        top_ref[side] = scr[side, :EDGE, :].astype(BF16)
        bot_ref[side] = scr[side, rows - EDGE :, :].astype(BF16)


def pack(par, tokens):
    lev, lat, lon, d = tokens.shape
    main = (lat - 2 * SHIFT_LAT) * ROW
    return pl.pallas_call(
        pack_kernel,
        in_specs=[pl.BlockSpec(memory_space=pltpu.SMEM)] + vmem(1),
        out_specs=vmem(4),
        out_shape=[
            jax.ShapeDtypeStruct((main, d), BF16),
            jax.ShapeDtypeStruct((main, d), BF16),
            jax.ShapeDtypeStruct((2, EDGE, d), BF16),
            jax.ShapeDtypeStruct((2, EDGE, d), BF16),
        ],
        scratch_shapes=[pltpu.VMEM((2, lat * ROW, d), F32)],
        compiler_params=params(),
        name="pack",
    )(par, tokens)


def unpack_kernel(par_ref, near_ref, far_ref, edge_ref, out_ref, scr):
    lev, lat = out_ref.shape[0], out_ref.shape[1]
    par = par_ref[0]
    rows = lat * ROW
    mid = near_ref.shape[0]
    scr[0, EDGE : EDGE + mid, :] = near_ref[...].astype(F32)
    scr[1, EDGE : EDGE + mid, :] = far_ref[...].astype(F32)
    for side in range(2):
        part = edge_ref[side].astype(F32)
        scr[side, :EDGE, :] = part[4 : 4 + EDGE]
        scr[side, rows - EDGE :, :] = part[4 + EDGE : 4 + 2 * EDGE]
    for h in range(lat):
        for z in range(lev):
            off = h * ROW + z * SHIFT_LON
            left = scr[1 - par, off : off + SHIFT_LON, :]
            right = scr[par, off : off + SHIFT_LON, :]
            out_ref[z, h] = jnp.concatenate([left, right], 0).astype(BF16)


def unpack(par, near, far, edge, shape):
    lev, lat, lon, d = shape
    return pl.pallas_call(
        unpack_kernel,
        in_specs=[pl.BlockSpec(memory_space=pltpu.SMEM)] + vmem(3),
        out_specs=vmem(1)[0],
        out_shape=jax.ShapeDtypeStruct(shape, BF16),
        scratch_shapes=[pltpu.VMEM((2, lat * ROW, d), F32)],
        compiler_params=params(),
        name="unpack",
    )(par, near, far, edge)


def bias_kernel(e_ref, out_ref):
    heads = out_ref.shape[1]
    out_ref[...] = jnp.zeros_like(out_ref)
    for h in range(WIN_LAT):
        start = (WIN_LAT - 1 - h) * ROW
        own = e_ref[0, :, :, start : start + HALF]
        for side in range(2):
            halo = e_ref[1 + side, :, :, start : start + HALF]
            out_ref[side, :, h * ROW : (h + 1) * ROW, :HALF] = own
            out_ref[side, :, h * ROW : (h + 1) * ROW, HALF:KEYS] = halo


def expand_bias(even, bias_table):
    heads = bias_table.shape[1]
    nz, nh, nw = 2 * WIN_LEV - 1, 2 * WIN_LAT - 1, 2 * WIN_LON - 1
    wide = 2 * SHIFT_LON - 1
    flip = (jnp.transpose(bias_table[::-1], (1, 0)) * LOG2E).reshape(heads, nz, nh, nw)
    flip = jnp.transpose(flip, (0, 2, 1, 3))
    mine = flip[..., SHIFT_LON : SHIFT_LON + wide]
    ahead = flip[..., 2 * SHIFT_LON : 2 * SHIFT_LON + wide]
    behind = flip[..., :wide]
    kinds = jnp.stack(
        [mine, jnp.where(even, ahead, behind), jnp.where(even, behind, ahead)]
    )
    parts = []
    for z in range(WIN_LEV):
        for w in range(SHIFT_LON):
            parts.append(
                kinds[
                    :,
                    :,
                    :,
                    WIN_LEV - 1 - z : 2 * WIN_LEV - 1 - z,
                    SHIFT_LON - 1 - w : 2 * SHIFT_LON - 1 - w,
                ].reshape(3, heads, nh * ROW)
            )
    spread = jnp.stack(parts, axis=2)
    return pl.pallas_call(
        bias_kernel,
        in_specs=vmem(1),
        out_specs=vmem(1)[0],
        out_shape=jax.ShapeDtypeStruct((2, heads, HALF, LANES), F32),
        compiler_params=params(),
        name="bias",
    )(spread)


def label_masks(even, group_ids, lat_start, lon_start, lat_rows, lon_cols):
    total_lat = group_ids.shape[0]
    rows = jnp.arange(total_lat, dtype=jnp.int32)
    label = group_ids * 2 + (rows >= total_lat - SHIFT_LAT).astype(jnp.int32)[:, None]
    label = jnp.concatenate([label[-2 * SHIFT_LAT :], label], 0)
    label = jnp.concatenate([label[:, -WIN_LON:], label], 1)
    part = lax.dynamic_slice(
        label, (lat_start, lon_start), (lat_rows + 2 * SHIFT_LAT, lon_cols + WIN_LON)
    )
    s = SHIFT_LON
    left = jnp.concatenate([part[:, s : 2 * s], part[:, :s]], 1)
    right = part[:, 2 * s :]
    sides = jnp.stack([jnp.where(even, right, left), jnp.where(even, left, right)])
    wins = sides.shape[1] // WIN_LAT
    sides = sides.reshape(2, wins, WIN_LAT, 2, 1, s)
    sides = jnp.broadcast_to(sides, (2, wins, WIN_LAT, 2, WIN_LEV, s))
    sides = jnp.transpose(sides, (0, 1, 3, 2, 4, 5)).reshape(2, wins, KEYS)
    keys = jnp.pad(sides, ((0, 0), (0, 0), (0, LANES - KEYS)), constant_values=-1)
    same = sides[:, :, :HALF, None] == keys[:, :, None, :]
    return jnp.where(same, 0.0, -jnp.inf).astype(F32)


def norm_rows(value, gain):
    mean = jnp.mean(value, -1, keepdims=True)
    centred = value - mean
    var = jnp.mean(centred * centred, -1, keepdims=True)
    return centred * lax.rsqrt(var + EPS) * gain


def gelu(x):
    return 0.5 * x * (1.0 + lax.erf(x * 0.7071067811865476))


def layer_kernel(
    sides, wins, q_lo, q_rows, *refs
):
    refs = list(refs)
    own = [refs.pop(0) for _ in range(sides)]
    halo = [refs.pop(0) for _ in range(sides)]
    mask_ref, bias_ref, w_qkv, w_proj, gain_attn, w_in, w_out, gain_mlp, out_ref = refs[:9]
    q_scr, k_scr, v_scr, o_scr, mid_scr, acc_scr = refs[9:]
    d = w_proj.shape[0]
    heads = bias_ref.shape[1]
    hd = d // heads
    lanes = GROUP * hd
    groups = heads // GROUP
    per = q_rows // wins
    scale = LOG2E / hd**0.5

    k_scr[:, KEYS:, :] = jnp.zeros((sides * wins, LANES - KEYS, d), BF16)
    v_scr[:, KEYS:, :] = jnp.zeros((sides * wins, LANES - KEYS, 2 * d), BF16)
    for g in range(groups):
        v_scr[:, :, (2 * g + 1) * lanes : (2 * g + 2) * lanes] = jnp.ones((sides * wins, LANES, lanes), BF16)
    step = 2 * lanes
    for s in range(sides):
        xq = own[s][...] if q_rows == own[s].shape[0] else own[s][q_lo : q_lo + q_rows, :]
        for c in range(0, d, step):
            q = jnp.dot(xq, w_qkv[:, c : c + step], preferred_element_type=F32)
            q_scr[s * q_rows : (s + 1) * q_rows, c : c + step] = q * scale
        for c in range(0, d, step):
            for base in (d, 2 * d):
                w = w_qkv[:, base + c : base + c + step]
                a = jnp.dot(own[s][...], w, preferred_element_type=F32)
                b = jnp.dot(halo[s][...], w, preferred_element_type=F32)
                for i in range(wins):
                    both = jnp.concatenate(
                        [a[i * HALF : (i + 1) * HALF], b[i * HALF : (i + 1) * HALF]], 0
                    ).astype(BF16)
                    if base == d:
                        k_scr[s * wins + i, :KEYS, c : c + step] = both
                    else:
                        v_scr[s * wins + i, :KEYS, 2 * c : 2 * c + lanes] = both[:, :lanes]
                        v_scr[s * wins + i, :KEYS, 2 * c + step : 2 * c + step + lanes] = both[:, lanes:]

    lane_head = lax.broadcasted_iota(jnp.int32, (per, lanes), 1) // hd

    def window(s, i):
        first = (q_lo + i * per) - i * HALF
        wi = s * wins + i
        qs = s * q_rows + i * per
        if not isinstance(i, int):
            qs = pl.multiple_of(qs, 8)
            first = 0
        mask = mask_ref[wi, first : first + per, :]
        mask = jnp.concatenate([mask] * GROUP, 0)
        for g in range(groups):
            q = q_scr[pl.ds(qs, per), g * lanes : (g + 1) * lanes]
            lhs = jnp.concatenate(
                [jnp.where(lane_head == j, q, 0.0) for j in range(GROUP)], 0
            ).astype(BF16)
            k = k_scr[wi, :, g * lanes : (g + 1) * lanes]
            sc = lax.dot_general(lhs, k, (((1,), (1,)), ((), ())), preferred_element_type=F32)
            bias = bias_ref[s, g * GROUP : (g + 1) * GROUP, first : first + per, :]
            sc = sc + bias.reshape(GROUP * per, LANES) + mask
            top = jnp.max(sc, -1, keepdims=True)
            p = jnp.exp2(sc - top).astype(BF16)
            o = jnp.dot(p, v_scr[wi, :, 2 * g * lanes : (2 * g + 2) * lanes], preferred_element_type=F32)
            num, den = o[:per, :lanes], o[:per, lanes:]
            for j in range(1, GROUP):
                here = lane_head == j
                num = jnp.where(here, o[j * per : (j + 1) * per, :lanes], num)
                den = jnp.where(here, o[j * per : (j + 1) * per, lanes:], den)
            o_scr[pl.ds(qs, per), g * lanes : (g + 1) * lanes] = num / den

    for s in range(sides):
        if per == HALF:
            lax.fori_loop(0, wins, lambda i, c, s=s: (window(s, i), c)[1], 0)
        else:
            for i in range(wins):
                window(s, i)

    total = sides * q_rows
    proj = jnp.dot(o_scr[...].astype(BF16), w_proj[...], preferred_element_type=F32)
    branch = norm_rows(proj, gain_attn[...]).astype(BF16).astype(F32)
    for s in range(sides):
        x = own[s][...] if q_rows == own[s].shape[0] else own[s][q_lo : q_lo + q_rows, :]
        mid_scr[s * q_rows : (s + 1) * q_rows, :] = (
            x.astype(F32) + branch[s * q_rows : (s + 1) * q_rows]
        ).astype(BF16)
    ff = w_in.shape[1]
    chunk = 256
    for c in range(0, ff, chunk):
        up = jnp.dot(mid_scr[...], w_in[:, c : c + chunk], preferred_element_type=F32)
        hid = gelu(up).astype(BF16)
        down = jnp.dot(hid, w_out[c : c + chunk, :], preferred_element_type=F32)
        if c == 0:
            acc_scr[...] = down
        else:
            acc_scr[...] += down
    res = mid_scr[...].astype(F32) + norm_rows(acc_scr[...], gain_mlp[...])
    for s in range(sides):
        part = res[s * q_rows : (s + 1) * q_rows].astype(BF16)
        if sides == 1:
            out_ref[...] = part
        else:
            out_ref[s] = part


def layer(name, own, halo, mask, bias, weights, q_lo, q_rows):
    sides = len(own)
    wins = own[0].shape[0] // HALF
    d = own[0].shape[1]
    shape = (q_rows, d) if sides == 1 else (sides, q_rows, d)
    total = sides * q_rows
    return pl.pallas_call(
        functools.partial(layer_kernel, sides, wins, q_lo, q_rows),
        in_specs=vmem(2 * sides + 2 + len(weights)),
        out_specs=vmem(1)[0],
        out_shape=jax.ShapeDtypeStruct(shape, BF16),
        scratch_shapes=[
            pltpu.VMEM((total, d), F32),
            pltpu.VMEM((sides * wins, LANES, d), BF16),
            pltpu.VMEM((sides * wins, LANES, 2 * d), BF16),
            pltpu.VMEM((total, d), F32),
            pltpu.VMEM((total, d), BF16),
            pltpu.VMEM((total, d), F32),
        ],
        compiler_params=params(),
        name=name,
    )(*own, *halo, mask, bias, *weights)


def per_device(tokens, group_ids, bias_table, w_qkv, w_proj, gain_attn, w_in, w_out, gain_mlp):
    lat_rows = tokens.shape[2]
    lon_cols = tokens.shape[3]
    lon_count = lax.axis_size("lon")
    lat_count = lax.axis_size("lat")
    lon_at = lax.axis_index("lon")
    par = lax.rem(lon_at, 2).astype(jnp.int32)
    even = par == 0
    near_pairs = [(i, i ^ 1) for i in range(lon_count)]
    far_pairs = [(i, (i + (1 if i % 2 else -1)) % lon_count) for i in range(lon_count)]
    down_pairs = [(i, (i + 1) % lat_count) for i in range(lat_count)]
    up_pairs = [(i, (i - 1) % lat_count) for i in range(lat_count)]

    near, far, top, bot = pack(par.reshape(1), tokens[0])
    far_halo = lax.ppermute(far, "lon", far_pairs)
    near_halo = lax.ppermute(near, "lon", near_pairs)
    above = lax.ppermute(bot, "lat", down_pairs)
    below = lax.ppermute(top, "lat", up_pairs)
    edge = [jnp.concatenate([above[s], top[s], bot[s], below[s]], 0) for s in range(2)]
    edge_halo = [
        lax.ppermute(edge[0], "lon", near_pairs),
        lax.ppermute(edge[1], "lon", far_pairs),
    ]
    bias = expand_bias(even, bias_table)
    mask = label_masks(
        even, group_ids, lax.axis_index("lat") * lat_rows, lon_at * lon_cols, lat_rows, lon_cols
    )
    wins = mask.shape[1]
    weights = [w_qkv, w_proj, gain_attn.reshape(1, -1), w_in, w_out, gain_mlp.reshape(1, -1)]
    rows = near.shape[0]
    res_near = layer("near", [near], [near_halo], mask[0, 1 : wins - 1], bias[:1], weights, 0, rows)
    res_far = layer("far", [far], [far_halo], mask[1, 1 : wins - 1], bias[1:], weights, 0, rows)
    edge_mask = jnp.stack([mask[:, 0], mask[:, wins - 1]], 1).reshape(4, HALF, LANES)
    res_edge = layer("edge", edge, edge_halo, edge_mask, bias, weights, 32, 80)
    out = unpack(par.reshape(1), res_near, res_far, res_edge, tokens.shape[1:])
    return out[None]


def solution(mesh):
    in_specs = (P(None, None, "lat", "lon", None), P(), P(), P(), P(), P(), P(), P(), P())
    out_specs = P(None, None, "lat", "lon", None)
    return jax.shard_map(
        per_device, mesh=mesh, in_specs=in_specs, out_specs=out_specs, check_vma=False
    )
```

```python
import functools

import jax
import jax.numpy as jnp
import numpy as np
from jax import lax
from jax.experimental import pallas as pl
from jax.experimental.pallas import tpu as pltpu
from jax.sharding import PartitionSpec as P

WIN_LEV = 2
WIN_LAT = 6
WIN_LON = 12
SHIFT_LAT = 3
SHIFT_LON = 6

EPS = 1e-05
LOG2E = 1.4426950408889634
HALF = WIN_LEV * WIN_LAT * SHIFT_LON
ROW = WIN_LEV * SHIFT_LON
EDGE = SHIFT_LAT * ROW
KEYS = 2 * HALF
LANES = 256
GROUP = 4
PACK_CHUNKS = 6
VMEM_LIMIT = 50 * 1024 * 1024

F32 = jnp.float32
BF16 = jnp.bfloat16


def params():
    return pltpu.CompilerParams(vmem_limit_bytes=VMEM_LIMIT)


def vmem(count):
    return [pl.BlockSpec(memory_space=pltpu.VMEM)] * count


def pack_kernel(par_ref, tok_ref, near_ref, far_ref, top_ref, bot_ref, buf, main, ends, sems):
    cells = tok_ref.shape[0]
    lat = main.shape[1] // ROW + 2 * SHIFT_LAT
    wide = cells // lat
    par = par_ref[0]
    each = cells // PACK_CHUNKS
    copies = [
        pltpu.make_async_copy(
            tok_ref.at[pl.ds(i * each, each)], buf.at[pl.ds(i * each, each)], sems.at[i]
        )
        for i in range(PACK_CHUNKS)
    ]
    for copy in copies:
        copy.start()
    waited = 0
    for h in range(lat):
        while waited < PACK_CHUNKS and waited * each < (h + 1) * wide:
            copies[waited].wait()
            waited += 1
        for half in range(2):
            at = h * wide + half * SHIFT_LON
            x = buf[at : at + SHIFT_LON].astype(F32).reshape(ROW, buf.shape[2])
            side = par if half else 1 - par
            if h < SHIFT_LAT:
                ends[side, h * ROW : (h + 1) * ROW, :] = x
            elif h >= lat - SHIFT_LAT:
                off = 40 + (h - lat + SHIFT_LAT) * ROW
                ends[side, off : off + ROW, :] = x
            else:
                off = (h - SHIFT_LAT) * ROW
                main[side, off : off + ROW, :] = x
    near_ref[...] = main[0].astype(BF16)
    far_ref[...] = main[1].astype(BF16)
    for side in range(2):
        top_ref[side] = ends[side, :EDGE, :].astype(BF16)
        bot_ref[side] = ends[side, 40 : 40 + EDGE, :].astype(BF16)


def pack(par, cells, lat):
    count, lev, d = cells.shape
    main = (lat - 2 * SHIFT_LAT) * ROW
    return pl.pallas_call(
        pack_kernel,
        in_specs=[pl.BlockSpec(memory_space=pltpu.SMEM), pl.BlockSpec(memory_space=pl.ANY)],
        out_specs=vmem(4),
        out_shape=[
            jax.ShapeDtypeStruct((main, d), BF16),
            jax.ShapeDtypeStruct((main, d), BF16),
            jax.ShapeDtypeStruct((2, EDGE, d), BF16),
            jax.ShapeDtypeStruct((2, EDGE, d), BF16),
        ],
        scratch_shapes=[
            pltpu.VMEM((count, lev, d), BF16),
            pltpu.VMEM((2, main, d), F32),
            pltpu.VMEM((2, 80, d), F32),
            pltpu.SemaphoreType.DMA((PACK_CHUNKS,)),
        ],
        compiler_params=params(),
        name="pack",
    )(par, cells)


def edge_pack_kernel(above_ref, top_ref, bot_ref, below_ref, near_ref, far_ref, scr):
    for side, out in enumerate((near_ref, far_ref)):
        for i, ref in enumerate((above_ref, top_ref, bot_ref, below_ref)):
            scr[i * EDGE : (i + 1) * EDGE, :] = ref[side].astype(F32)
        out[...] = scr[...].astype(BF16)


def edge_pack(above, top, bot, below):
    d = top.shape[2]
    return pl.pallas_call(
        edge_pack_kernel,
        in_specs=vmem(4),
        out_specs=vmem(2),
        out_shape=[jax.ShapeDtypeStruct((4 * EDGE, d), BF16)] * 2,
        scratch_shapes=[pltpu.VMEM((4 * EDGE, d), F32)],
        compiler_params=params(),
        name="edge_pack",
    )(above, top, bot, below)


def unpack_kernel(par_ref, near_ref, far_ref, edge_ref, out_ref, scr):
    par = par_ref[0]
    mid = near_ref.shape[0]
    rows = mid + 2 * EDGE
    lat = rows // ROW
    wide = out_ref.shape[0] // lat
    scr[0, EDGE : EDGE + mid, :] = near_ref[...].astype(F32)
    scr[1, EDGE : EDGE + mid, :] = far_ref[...].astype(F32)
    for side in range(2):
        part = edge_ref[side].astype(F32)
        scr[side, :EDGE, :] = part[4 : 4 + EDGE]
        scr[side, rows - EDGE :, :] = part[4 + EDGE : 4 + 2 * EDGE]
    for h in range(lat):
        for half in range(2):
            at = h * wide + half * SHIFT_LON
            side = par if half else 1 - par
            x = scr[side, h * ROW : (h + 1) * ROW, :]
            out_ref[at : at + SHIFT_LON] = x.reshape(SHIFT_LON, WIN_LEV, x.shape[1]).astype(BF16)


def unpack(par, near, far, edge, cells):
    d = near.shape[1]
    return pl.pallas_call(
        unpack_kernel,
        in_specs=[pl.BlockSpec(memory_space=pltpu.SMEM)] + vmem(3),
        out_specs=vmem(1)[0],
        out_shape=jax.ShapeDtypeStruct((cells, WIN_LEV, d), BF16),
        scratch_shapes=[pltpu.VMEM((2, near.shape[0] + 2 * EDGE, d), F32)],
        compiler_params=params(),
        name="unpack",
    )(par, near, far, edge)


def spread_matrix(count):
    nw, nh = 2 * WIN_LON - 1, 2 * WIN_LAT - 1
    out = np.zeros((count, 3, LANES), np.float32)
    for kind, centre in enumerate((WIN_LON - 1, SHIFT_LON - 1, WIN_LON + SHIFT_LON - 1)):
        for j in range(nh):
            for w in range(SHIFT_LON):
                for z in range(WIN_LEV):
                    at = (WIN_LEV - 1 - z) * nh * nw + (nh - 1 - j) * nw + centre - w
                    out[at, kind, j * ROW + w * WIN_LEV + z] = 1
    return out.reshape(count, 3 * LANES)


def prep_kernel(
    at_ref, gid_ref, table_ref, spread_ref, bias_near, bias_far, mask_near, mask_far, mask_edge, wide, kinds
):
    heads, offsets = table_ref.shape
    nw, nh = 2 * WIN_LON - 1, 2 * WIN_LAT - 1
    par, lat_at, lon_at = at_ref[0], at_ref[1], at_ref[2]
    count = wide.shape[1]
    wide[...] = jnp.zeros_like(wide)
    wide[:, :offsets] = table_ref[...] * LOG2E
    x = jnp.broadcast_to(wide[...][:, None, :], (heads, 16, count)).reshape(heads * 16, count)
    place = lax.broadcasted_iota(jnp.int32, x.shape, 0) % 16
    for amount, bit in ((nh * nw, place % 2), (1, place // 2 % 2), (2, place // 4 % 2), (4, place // 8)):
        x = jnp.where(bit == 1, pltpu.roll(x, count - amount, 1), x)
    high = x.astype(BF16)
    low = (x - high.astype(F32)).astype(BF16)
    for kind in range(3):
        m = spread_ref[:, kind * LANES : (kind + 1) * LANES]
        y = jnp.dot(high, m, preferred_element_type=F32) + jnp.dot(low, m, preferred_element_type=F32)
        kinds[kind] = y.reshape(heads, 16, LANES)
    for side, out in enumerate((bias_near, bias_far)):
        halo = kinds[2 - par if side else 1 + par]
        out[:, :, KEYS:] = jnp.zeros((heads, HALF, LANES - KEYS), F32)
        for h in range(WIN_LAT):
            start = (WIN_LAT - 1 - h) * ROW
            out[:, h * ROW : (h + 1) * ROW, :HALF] = kinds[0, :, :ROW, start : start + HALF]
            out[:, h * ROW : (h + 1) * ROW, HALF:KEYS] = halo[:, :ROW, start : start + HALF]
    total, around = gid_ref.shape
    wins = mask_near.shape[0] + 2
    lat_rows = (wins - 1) * WIN_LAT
    lane = lax.broadcasted_iota(jnp.int32, (1, LANES), 1)
    is_halo = lane >= HALF
    rest = jnp.where(is_halo, lane - HALF, lane)
    h_of = rest // ROW
    w_of = rest % ROW // WIN_LEV
    ids = gid_ref[...].astype(BF16)
    row = lax.broadcasted_iota(jnp.int32, (total, LANES), 0)
    col = lax.broadcasted_iota(jnp.int32, (around, LANES), 0)
    for side in range(2):
        right = par == side
        offset = jnp.where(
            right, jnp.where(is_halo, SHIFT_LON, 0), jnp.where(is_halo, -WIN_LON, -SHIFT_LON)
        )
        want = lon_at * 2 * SHIFT_LON + offset + w_of
        want = jnp.where(want < 0, want + around, want)
        pick = jnp.where(col == want, 1.0, 0.0).astype(BF16)
        label = 2.0 * jnp.dot(ids, pick, preferred_element_type=F32)
        label = label + jnp.where(row >= total - SHIFT_LAT, 1.0, 0.0)
        lines = []
        for k in range(wins):
            want = lat_at * lat_rows + (k - 1) * WIN_LAT + h_of
            want = jnp.where(want < 0, want + total, want)
            line = jnp.sum(jnp.where(row == want, label, 0.0), 0, keepdims=True)
            lines.append(jnp.where(lane < KEYS, line, -1.0))
        lines = jnp.concatenate(lines, 0)
        cols = lines[:, :128].T
        for k in range(wins):
            same = cols[:HALF, k : k + 1] == lines[k : k + 1, :]
            mask = jnp.where(same, 0.0, -jnp.inf)
            if k == 0:
                mask_edge[2 * side] = mask
            elif k == wins - 1:
                mask_edge[2 * side + 1] = mask
            elif side == 0:
                mask_near[k - 1] = mask
            else:
                mask_far[k - 1] = mask


def prep(at, group_ids, table, wins):
    heads, offsets = table.shape
    count = -(-offsets // LANES) * LANES
    spread = jnp.asarray(spread_matrix(count), BF16)
    return pl.pallas_call(
        prep_kernel,
        in_specs=[pl.BlockSpec(memory_space=pltpu.SMEM)] + vmem(3),
        out_specs=vmem(5),
        out_shape=[jax.ShapeDtypeStruct((heads, HALF, LANES), F32)] * 2
        + [jax.ShapeDtypeStruct((wins - 2, HALF, LANES), F32)] * 2
        + [jax.ShapeDtypeStruct((4, HALF, LANES), F32)],
        scratch_shapes=[
            pltpu.VMEM((heads, count), F32),
            pltpu.VMEM((3, heads, 16, LANES), F32),
        ],
        compiler_params=params(),
        name="prep",
    )(at, group_ids, table, spread)


def norm_rows(value, gain):
    mean = jnp.mean(value, -1, keepdims=True)
    centred = value - mean
    var = jnp.mean(centred * centred, -1, keepdims=True)
    return centred * lax.rsqrt(var + EPS) * gain


def gelu(x):
    return 0.5 * x * (1.0 + lax.erf(x * 0.7071067811865476))


def layer_kernel(
    sides, wins, q_lo, q_rows, *refs
):
    refs = list(refs)
    own = [refs.pop(0) for _ in range(sides)]
    halo = [refs.pop(0) for _ in range(sides)]
    bias = [refs.pop(0) for _ in range(sides)]
    mask_ref, w_qkv, w_proj, gain_attn, w_in, w_out, gain_mlp, out_ref = refs[:8]
    q_scr, k_scr, v_scr, o_scr, mid_scr, acc_scr = refs[8:]
    d = w_proj.shape[0]
    heads = bias[0].shape[0]
    hd = d // heads
    lanes = GROUP * hd
    groups = heads // GROUP
    per = q_rows // wins
    scale = LOG2E / hd**0.5

    k_scr[:, KEYS:, :] = jnp.zeros((sides * wins, LANES - KEYS, d), BF16)
    v_scr[:, KEYS:, :] = jnp.zeros((sides * wins, LANES - KEYS, 2 * d), BF16)
    for g in range(groups):
        v_scr[:, :, (2 * g + 1) * lanes : (2 * g + 2) * lanes] = jnp.ones((sides * wins, LANES, lanes), BF16)
    step = 2 * lanes
    for s in range(sides):
        xq = own[s][...] if q_rows == own[s].shape[0] else own[s][q_lo : q_lo + q_rows, :]
        for c in range(0, d, step):
            q = jnp.dot(xq, w_qkv[:, c : c + step], preferred_element_type=F32)
            q_scr[s * q_rows : (s + 1) * q_rows, c : c + step] = q * scale
        for c in range(0, d, step):
            for base in (d, 2 * d):
                w = w_qkv[:, base + c : base + c + step]
                a = jnp.dot(own[s][...], w, preferred_element_type=F32)
                b = jnp.dot(halo[s][...], w, preferred_element_type=F32)
                for i in range(wins):
                    both = jnp.concatenate(
                        [a[i * HALF : (i + 1) * HALF], b[i * HALF : (i + 1) * HALF]], 0
                    ).astype(BF16)
                    if base == d:
                        k_scr[s * wins + i, :KEYS, c : c + step] = both
                    else:
                        v_scr[s * wins + i, :KEYS, 2 * c : 2 * c + lanes] = both[:, :lanes]
                        v_scr[s * wins + i, :KEYS, 2 * c + step : 2 * c + step + lanes] = both[:, lanes:]

    lane_head = lax.broadcasted_iota(jnp.int32, (per, lanes), 1) // hd

    def window(s, i):
        first = (q_lo + i * per) - i * HALF
        wi = s * wins + i
        qs = s * q_rows + i * per
        if not isinstance(i, int):
            qs = pl.multiple_of(qs, 8)
            first = 0
        mask = mask_ref[wi, first : first + per, :]
        mask = jnp.concatenate([mask] * GROUP, 0)
        for g in range(groups):
            q = q_scr[pl.ds(qs, per), g * lanes : (g + 1) * lanes]
            lhs = jnp.concatenate(
                [jnp.where(lane_head == j, q, 0.0) for j in range(GROUP)], 0
            ).astype(BF16)
            k = k_scr[wi, :, g * lanes : (g + 1) * lanes]
            sc = lax.dot_general(lhs, k, (((1,), (1,)), ((), ())), preferred_element_type=F32)
            extra = bias[s][g * GROUP : (g + 1) * GROUP, first : first + per, :]
            sc = sc + extra.reshape(GROUP * per, LANES) + mask
            top = jnp.max(sc, -1, keepdims=True)
            p = jnp.exp2(sc - top).astype(BF16)
            o = jnp.dot(p, v_scr[wi, :, 2 * g * lanes : (2 * g + 2) * lanes], preferred_element_type=F32)
            num, den = o[:per, :lanes], o[:per, lanes:]
            for j in range(1, GROUP):
                here = lane_head == j
                num = jnp.where(here, o[j * per : (j + 1) * per, :lanes], num)
                den = jnp.where(here, o[j * per : (j + 1) * per, lanes:], den)
            o_scr[pl.ds(qs, per), g * lanes : (g + 1) * lanes] = num / den

    for s in range(sides):
        if per == HALF:
            lax.fori_loop(0, wins, lambda i, c, s=s: (window(s, i), c)[1], 0)
        else:
            for i in range(wins):
                window(s, i)

    total = sides * q_rows
    proj = jnp.dot(o_scr[...].astype(BF16), w_proj[...], preferred_element_type=F32)
    branch = norm_rows(proj, gain_attn[...]).astype(BF16).astype(F32)
    for s in range(sides):
        x = own[s][...] if q_rows == own[s].shape[0] else own[s][q_lo : q_lo + q_rows, :]
        mid_scr[s * q_rows : (s + 1) * q_rows, :] = (
            x.astype(F32) + branch[s * q_rows : (s + 1) * q_rows]
        ).astype(BF16)
    ff = w_in.shape[1]
    chunk = 256
    for c in range(0, ff, chunk):
        up = jnp.dot(mid_scr[...], w_in[:, c : c + chunk], preferred_element_type=F32)
        hid = gelu(up).astype(BF16)
        down = jnp.dot(hid, w_out[c : c + chunk, :], preferred_element_type=F32)
        if c == 0:
            acc_scr[...] = down
        else:
            acc_scr[...] += down
    res = mid_scr[...].astype(F32) + norm_rows(acc_scr[...], gain_mlp[...])
    for s in range(sides):
        part = res[s * q_rows : (s + 1) * q_rows].astype(BF16)
        if sides == 1:
            out_ref[...] = part
        else:
            out_ref[s] = part


def layer(name, own, halo, bias, mask, weights, q_lo, q_rows):
    sides = len(own)
    wins = own[0].shape[0] // HALF
    d = own[0].shape[1]
    shape = (q_rows, d) if sides == 1 else (sides, q_rows, d)
    total = sides * q_rows
    return pl.pallas_call(
        functools.partial(layer_kernel, sides, wins, q_lo, q_rows),
        in_specs=vmem(3 * sides + 1 + len(weights)),
        out_specs=vmem(1)[0],
        out_shape=jax.ShapeDtypeStruct(shape, BF16),
        scratch_shapes=[
            pltpu.VMEM((total, d), F32),
            pltpu.VMEM((sides * wins, LANES, d), BF16),
            pltpu.VMEM((sides * wins, LANES, 2 * d), BF16),
            pltpu.VMEM((total, d), F32),
            pltpu.VMEM((total, d), BF16),
            pltpu.VMEM((total, d), F32),
        ],
        compiler_params=params(),
        name=name,
    )(*own, *halo, *bias, mask, *weights)


def per_device(tokens, group_ids, bias_table, w_qkv, w_proj, gain_attn, w_in, w_out, gain_mlp):
    samples, lev, lat_rows, lon_cols, d = tokens.shape
    lon_count = lax.axis_size("lon")
    lat_count = lax.axis_size("lat")
    lon_at = lax.axis_index("lon").astype(jnp.int32)
    lat_at = lax.axis_index("lat").astype(jnp.int32)
    par = lax.rem(lon_at, 2)
    near_pairs = [(i, i ^ 1) for i in range(lon_count)]
    far_pairs = [(i, (i + (1 if i % 2 else -1)) % lon_count) for i in range(lon_count)]
    down_pairs = [(i, (i + 1) % lat_count) for i in range(lat_count)]
    up_pairs = [(i, (i - 1) % lat_count) for i in range(lat_count)]
    at = jnp.stack([par, lat_at, lon_at])
    wins = lat_rows // WIN_LAT + 1

    cells = jnp.transpose(tokens[0], (1, 2, 0, 3)).reshape(lat_rows * lon_cols, lev, d)
    near, far, top, bot = pack(at, cells, lat_rows)
    far_halo = lax.ppermute(far, "lon", far_pairs)
    near_halo = lax.ppermute(near, "lon", near_pairs)
    above = lax.ppermute(bot, "lat", down_pairs)
    below = lax.ppermute(top, "lat", up_pairs)
    bias_near, bias_far, mask_near, mask_far, mask_edge = prep(at, group_ids, bias_table.T, wins)
    above, below, bias_near = lax.optimization_barrier((above, below, bias_near))
    edge_near, edge_far = edge_pack(above, top, bot, below)
    halo_edge_near = lax.ppermute(edge_near, "lon", near_pairs)
    halo_edge_far = lax.ppermute(edge_far, "lon", far_pairs)
    weights = [w_qkv, w_proj, gain_attn.reshape(1, -1), w_in, w_out, gain_mlp.reshape(1, -1)]
    rows = near.shape[0]
    near, edge_near = lax.optimization_barrier((near, edge_near))
    res_near = layer("near", [near], [near_halo], [bias_near], mask_near, weights, 0, rows)
    far, res_near = lax.optimization_barrier((far, res_near))
    res_far = layer("far", [far], [far_halo], [bias_far], mask_far, weights, 0, rows)
    edge_near, res_far = lax.optimization_barrier((edge_near, res_far))
    res_edge = layer(
        "edge",
        [edge_near, edge_far],
        [halo_edge_near, halo_edge_far],
        [bias_near, bias_far],
        mask_edge,
        weights,
        32,
        80,
    )
    out = unpack(at, res_near, res_far, res_edge, lat_rows * lon_cols)
    return jnp.transpose(out.reshape(lat_rows, lon_cols, lev, d), (2, 0, 1, 3))[None]


def solution(mesh):
    in_specs = (P(None, None, "lat", "lon", None), P(), P(), P(), P(), P(), P(), P(), P())
    out_specs = P(None, None, "lat", "lon", None)
    return jax.shard_map(
        per_device, mesh=mesh, in_specs=in_specs, out_specs=out_specs, check_vma=False
    )
```

```python
import functools

import jax
import jax.numpy as jnp
import numpy as np
from jax import lax
from jax.experimental import pallas as pl
from jax.experimental.pallas import tpu as pltpu
from jax.sharding import PartitionSpec as P

WIN_LEV = 2
WIN_LAT = 6
WIN_LON = 12
SHIFT_LAT = 3
SHIFT_LON = 6

EPS = 1e-05
LOG2E = 1.4426950408889634
HALF = WIN_LEV * WIN_LAT * SHIFT_LON
ROW = WIN_LEV * SHIFT_LON
EDGE = SHIFT_LAT * ROW
KEYS = 2 * HALF
SPREAD = 256
GROUP = 4
VMEM_LIMIT = 24 * 1024 * 1024
PACK_LIMIT = 20 * 1024 * 1024

F32 = jnp.float32
BF16 = jnp.bfloat16


def params(limit=VMEM_LIMIT):
    return pltpu.CompilerParams(vmem_limit_bytes=limit)


def cost(micros):
    return pl.CostEstimate(flops=int(micros * 1e9), bytes_accessed=int(micros * 3e6), transcendentals=0)


def anywhere(count):
    return [pl.BlockSpec(memory_space=pl.ANY)] * count


def vmem(count):
    return [pl.BlockSpec(memory_space=pltpu.VMEM)] * count


def pack_kernel(par_ref, tok_ref, near_ref, far_ref, top_ref, bot_ref):
    lat, d = tok_ref.shape[0], tok_ref.shape[-1]
    par = par_ref[0]
    for side, out in ((1, far_ref), (0, near_ref)):
        half = par if side else 1 - par
        out[...] = tok_ref[SHIFT_LAT : lat - SHIFT_LAT, half].reshape(out.shape)
        top_ref[side] = tok_ref[:SHIFT_LAT, half].reshape(EDGE, d)
        bot_ref[side] = tok_ref[lat - SHIFT_LAT :, half].reshape(EDGE, d)


def pack(par, cells):
    lat, _, lon, lev, d = cells.shape
    main = (lat - 2 * SHIFT_LAT) * ROW
    return pl.pallas_call(
        pack_kernel,
        in_specs=[pl.BlockSpec(memory_space=pltpu.SMEM)] + vmem(1),
        out_specs=vmem(4),
        out_shape=[
            jax.ShapeDtypeStruct((main, d), BF16),
            jax.ShapeDtypeStruct((main, d), BF16),
            jax.ShapeDtypeStruct((2, EDGE, d), BF16),
            jax.ShapeDtypeStruct((2, EDGE, d), BF16),
        ],
        compiler_params=params(PACK_LIMIT),
        cost_estimate=cost(1),
        name="pack",
    )(par, cells)


def edge_pack_kernel(above_ref, top_ref, bot_ref, below_ref, near_ref, far_ref, scr):
    for side, out in enumerate((near_ref, far_ref)):
        for i, ref in enumerate((above_ref, top_ref, bot_ref, below_ref)):
            scr[i * EDGE : (i + 1) * EDGE, :] = ref[side].astype(F32)
        out[...] = scr[...].astype(BF16)


def edge_pack(above, top, bot, below):
    d = top.shape[2]
    return pl.pallas_call(
        edge_pack_kernel,
        in_specs=vmem(4),
        out_specs=vmem(2),
        out_shape=[jax.ShapeDtypeStruct((4 * EDGE, d), BF16)] * 2,
        scratch_shapes=[pltpu.VMEM((4 * EDGE, d), F32)],
        compiler_params=params(),
        name="edge_pack",
    )(above, top, bot, below)


def spread_matrix(count):
    nw, nh = 2 * WIN_LON - 1, 2 * WIN_LAT - 1
    out = np.zeros((count, 3, SPREAD), np.float32)
    for kind, centre in enumerate((WIN_LON - 1, SHIFT_LON - 1, WIN_LON + SHIFT_LON - 1)):
        for j in range(nh):
            for w in range(SHIFT_LON):
                for z in range(WIN_LEV):
                    at = (WIN_LEV - 1 - z) * nh * nw + (nh - 1 - j) * nw + centre - w
                    out[at, kind, j * ROW + w * WIN_LEV + z] = 1
    return out.reshape(count, 3 * SPREAD)


def prep_kernel(
    at_ref,
    gid_any,
    table_any,
    spread_any,
    bias_near,
    bias_far,
    mask_near,
    mask_far,
    mask_edge,
    wide,
    kinds,
    gid_ref,
    table_ref,
    spread_ref,
    sems,
):
    pairs = ((table_any, table_ref), (gid_any, gid_ref), (spread_any, spread_ref))
    copies = [pltpu.make_async_copy(src, dst, sems.at[i]) for i, (src, dst) in enumerate(pairs)]
    for copy in copies:
        copy.start()
    heads, offsets = table_ref.shape
    nw, nh = 2 * WIN_LON - 1, 2 * WIN_LAT - 1
    par, lat_at, lon_at = at_ref[0], at_ref[1], at_ref[2]
    count = wide.shape[1]
    wide[...] = jnp.zeros_like(wide)
    copies[0].wait()
    wide[:, :offsets] = table_ref[...] * LOG2E
    x = jnp.broadcast_to(wide[...][:, None, :], (heads, 16, count)).reshape(heads * 16, count)
    place = lax.broadcasted_iota(jnp.int32, x.shape, 0) % 16
    for amount, bit in ((nh * nw, place % 2), (1, place // 2 % 2), (2, place // 4 % 2), (4, place // 8)):
        x = jnp.where(bit == 1, pltpu.roll(x, count - amount, 1), x)
    high = x.astype(BF16)
    low = (x - high.astype(F32)).astype(BF16)
    copies[2].wait()
    for kind in range(3):
        m = spread_ref[:, kind * SPREAD : (kind + 1) * SPREAD]
        y = jnp.dot(high, m, preferred_element_type=F32) + jnp.dot(low, m, preferred_element_type=F32)
        kinds[kind] = y.reshape(heads, 16, SPREAD)
    for side, out in enumerate((bias_near, bias_far)):
        halo = kinds[2 - par if side else 1 + par]
        for h in range(WIN_LAT):
            start = (WIN_LAT - 1 - h) * ROW
            out[:, h * ROW : (h + 1) * ROW, :HALF] = kinds[0, :, :ROW, start : start + HALF]
            out[:, h * ROW : (h + 1) * ROW, HALF:KEYS] = halo[:, :ROW, start : start + HALF]
    copies[1].wait()
    total, around = gid_ref.shape
    wins = mask_near.shape[0] + 2
    lat_rows = (wins - 1) * WIN_LAT
    lane = lax.broadcasted_iota(jnp.int32, (1, KEYS), 1)
    is_halo = lane >= HALF
    rest = jnp.where(is_halo, lane - HALF, lane)
    h_of = rest // ROW
    w_of = rest % ROW // WIN_LEV
    ids = gid_ref[...].astype(BF16)
    row = lax.broadcasted_iota(jnp.int32, (total, KEYS), 0)
    col = lax.broadcasted_iota(jnp.int32, (around, KEYS), 0)
    for side in range(2):
        right = par == side
        offset = jnp.where(
            right, jnp.where(is_halo, SHIFT_LON, 0), jnp.where(is_halo, -WIN_LON, -SHIFT_LON)
        )
        want = lon_at * 2 * SHIFT_LON + offset + w_of
        want = jnp.where(want < 0, want + around, want)
        pick = jnp.where(col == want, 1.0, 0.0).astype(BF16)
        label = 2.0 * jnp.dot(ids, pick, preferred_element_type=F32)
        label = label + jnp.where(row >= total - SHIFT_LAT, 1.0, 0.0)
        lines = []
        for k in range(wins):
            want = lat_at * lat_rows + (k - 1) * WIN_LAT + h_of
            want = jnp.where(want < 0, want + total, want)
            line = jnp.sum(jnp.where(row == want, label, 0.0), 0, keepdims=True)
            lines.append(line)
        lines = jnp.concatenate(lines, 0)
        cols = lines[:, :128].T
        for k in range(wins):
            same = cols[:HALF, k : k + 1] == lines[k : k + 1, :]
            mask = jnp.where(same, 0.0, -jnp.inf)
            if k == 0:
                mask_edge[2 * side] = mask
            elif k == wins - 1:
                mask_edge[2 * side + 1] = mask
            elif side == 0:
                mask_near[k - 1] = mask
            else:
                mask_far[k - 1] = mask


def prep(at, group_ids, table, wins):
    heads, offsets = table.shape
    count = -(-offsets // 256) * 256
    spread = jnp.asarray(spread_matrix(count), BF16)
    return pl.pallas_call(
        prep_kernel,
        in_specs=[pl.BlockSpec(memory_space=pltpu.SMEM)] + anywhere(3),
        out_specs=vmem(5),
        out_shape=[jax.ShapeDtypeStruct((heads, HALF, KEYS), F32)] * 2
        + [jax.ShapeDtypeStruct((wins - 2, HALF, KEYS), F32)] * 2
        + [jax.ShapeDtypeStruct((4, HALF, KEYS), F32)],
        scratch_shapes=[
            pltpu.VMEM((heads, count), F32),
            pltpu.VMEM((3, heads, 16, SPREAD), F32),
            pltpu.VMEM(group_ids.shape, jnp.int32),
            pltpu.VMEM(table.shape, F32),
            pltpu.VMEM(spread.shape, BF16),
            pltpu.SemaphoreType.DMA((3,)),
        ],
        compiler_params=params(),
        cost_estimate=cost(5),
        name="prep",
    )(at, group_ids, table, spread)


def norm_rows(value, gain):
    mean = jnp.mean(value, -1, keepdims=True)
    centred = value - mean
    var = jnp.mean(centred * centred, -1, keepdims=True)
    return centred * lax.rsqrt(var + EPS) * gain


def gelu(x):
    return 0.5 * x * (1.0 + lax.erf(x * 0.7071067811865476))


def attend(q, k, v, extra, mask, lane_head, hd):
    per, lanes = q.shape
    lhs = jnp.concatenate([jnp.where(lane_head == j, q, 0.0) for j in range(GROUP)], 0).astype(BF16)
    sc = lax.dot_general(lhs, k, (((1,), (1,)), ((), ())), preferred_element_type=F32)
    sc = sc + extra.reshape(GROUP * per, KEYS) + mask
    top = jnp.max(sc, -1, keepdims=True)
    p = jnp.exp2(sc - top).astype(BF16)
    o = jnp.dot(p, v, preferred_element_type=F32)
    num, den = o[:per, :lanes], o[:per, lanes:]
    for j in range(1, GROUP):
        here = lane_head == j
        num = jnp.where(here, o[j * per : (j + 1) * per, :lanes], num)
        den = jnp.where(here, o[j * per : (j + 1) * per, lanes:], den)
    return num / den


def layer_body(blocks, weights, scratch):
    w_qkv, w_proj, w_in, w_out, gain_attn, gain_mlp = weights
    q_scr, k_scr, v_scr, o_scr, mid_scr, acc_scr = scratch
    d = w_proj.shape[0]
    heads = blocks[0][2].shape[0]
    hd = d // heads
    lanes = GROUP * hd
    groups = heads // GROUP
    scale = LOG2E / hd**0.5
    step = 2 * lanes
    wi = 0
    for g in range(groups):
        ones = jnp.ones((v_scr.shape[0], KEYS, lanes), BF16)
        v_scr[:, :, (2 * g + 1) * lanes : (2 * g + 2) * lanes] = ones
    base = 0
    for own, halo, bias, mask_ref, mask_at, q_lo, q_rows in blocks:
        wins = own.shape[0] // HALF
        per = q_rows // wins
        for c in range(0, d, step):
            q = jnp.dot(own[q_lo : q_lo + q_rows, :], w_qkv[:, c : c + step], preferred_element_type=F32)
            q_scr[base : base + q_rows, c : c + step] = q * scale
            for part in (d, 2 * d):
                w = w_qkv[:, part + c : part + c + step]
                a = jnp.dot(own[...], w, preferred_element_type=F32)
                b = jnp.dot(halo[...], w, preferred_element_type=F32)
                for i in range(wins):
                    both = jnp.concatenate(
                        [a[i * HALF : (i + 1) * HALF], b[i * HALF : (i + 1) * HALF]], 0
                    ).astype(BF16)
                    if part == d:
                        k_scr[wi + i, :, c : c + step] = both
                    else:
                        v_scr[wi + i, :, 2 * c : 2 * c + lanes] = both[:, :lanes]
                        v_scr[wi + i, :, 2 * c + step : 2 * c + step + lanes] = both[:, lanes:]
        lane_head = lax.broadcasted_iota(jnp.int32, (per, lanes), 1) // hd
        for i in range(wins):
            first = q_lo + i * per - i * HALF
            at = base + i * per
            mask = jnp.concatenate([mask_ref[mask_at + i, first : first + per, :]] * GROUP, 0)
            for g in range(groups):
                o_scr[at : at + per, g * lanes : (g + 1) * lanes] = attend(
                    q_scr[at : at + per, g * lanes : (g + 1) * lanes],
                    k_scr[wi + i, :, g * lanes : (g + 1) * lanes],
                    v_scr[wi + i, :, 2 * g * lanes : (2 * g + 2) * lanes],
                    bias[g * GROUP : (g + 1) * GROUP, first : first + per, :],
                    mask,
                    lane_head,
                    hd,
                )
        base += q_rows
        wi += wins
    proj = jnp.dot(o_scr[...].astype(BF16), w_proj[...], preferred_element_type=F32)
    branch = norm_rows(proj, gain_attn[...]).astype(BF16).astype(F32)
    base = 0
    for own, _, _, _, _, q_lo, q_rows in blocks:
        mid_scr[base : base + q_rows, :] = (
            own[q_lo : q_lo + q_rows, :].astype(F32) + branch[base : base + q_rows]
        ).astype(BF16)
        base += q_rows
    ff = w_in.shape[1]
    chunk = 256
    for c in range(0, ff, chunk):
        up = jnp.dot(mid_scr[...], w_in[:, c : c + chunk], preferred_element_type=F32)
        hid = gelu(up).astype(BF16)
        down = jnp.dot(hid, w_out[c : c + chunk, :], preferred_element_type=F32)
        if c == 0:
            acc_scr[...] = down
        else:
            acc_scr[...] += down
    return mid_scr[...].astype(F32) + norm_rows(acc_scr[...], gain_mlp[...])


def near_kernel(own, halo, bias, mask, *refs):
    weights, out, scratch = refs[:6], refs[6], refs[7:]
    rows, d = own.shape
    res = layer_body([(own, halo, bias, mask, 0, 0, rows)], weights, scratch)
    out[...] = res.reshape(out.shape).astype(BF16)


def last_kernel(
    par_ref, near_res, far, far_halo, e_near, e_near_halo, e_far, e_far_halo, *refs
):
    bias_near, bias_far, mask_far, mask_edge = refs[:4]
    weights, out, near_sem, sems, far_buf, edge_buf = refs[4:10], *refs[10:15]
    scratch = refs[15:]
    par = par_ref[0]
    lat = out.shape[0]
    halves = (1 - par, par)
    main = pl.ds(SHIFT_LAT, lat - 2 * SHIFT_LAT)
    first = pltpu.make_async_copy(near_res, out.at[main, halves[0]], near_sem)
    first.start()
    rows = far.shape[0]
    lo, keep = EDGE // 8 * 8, 80
    res = layer_body(
        [
            (far, far_halo, bias_far, mask_far, 0, 0, rows),
            (e_near, e_near_halo, bias_near, mask_edge, 0, lo, keep),
            (e_far, e_far_halo, bias_far, mask_edge, 2, lo, keep),
        ],
        weights,
        scratch,
    )
    far_buf[...] = res[:rows].reshape(far_buf.shape).astype(BF16)
    copies = [pltpu.make_async_copy(far_buf, out.at[main, halves[1]], sems.at[4])]
    copies[0].start()
    shape = edge_buf.shape[2:]
    for side in range(2):
        at = rows + side * keep + EDGE - lo
        for end in range(2):
            part = res[at + end * EDGE : at + (end + 1) * EDGE]
            edge_buf[side, end] = part.reshape(shape).astype(BF16)
            place = pl.ds(end * (lat - SHIFT_LAT), SHIFT_LAT)
            copies.append(
                pltpu.make_async_copy(
                    edge_buf.at[side, end], out.at[place, halves[side]], sems.at[2 * side + end]
                )
            )
            copies[-1].start()
    for copy in copies:
        copy.wait()
    first.wait()


def layer_scratch(total, windows, weights):
    d = weights[1].shape[0]
    return [
        pltpu.VMEM((total, d), F32),
        pltpu.VMEM((windows, KEYS, d), BF16),
        pltpu.VMEM((windows, KEYS, 2 * d), BF16),
        pltpu.VMEM((total, d), F32),
        pltpu.VMEM((total, d), BF16),
        pltpu.VMEM((total, d), F32),
    ]


def near_layer(own, halo, bias, mask, weights):
    rows, d = own.shape
    shape = (rows // ROW, SHIFT_LON, WIN_LEV, d)
    return pl.pallas_call(
        near_kernel,
        in_specs=vmem(10),
        out_specs=vmem(1)[0],
        out_shape=jax.ShapeDtypeStruct(shape, BF16),
        scratch_shapes=layer_scratch(rows, rows // HALF, weights),
        compiler_params=params(),
        cost_estimate=cost(8),
        name="near",
    )(own, halo, bias, mask, *weights)


def last_layer(par, near_res, far, far_halo, edges, bias, masks, weights):
    rows, d = far.shape
    lat = rows // ROW + 2 * SHIFT_LAT
    shape = (lat, 2, SHIFT_LON, WIN_LEV, d)
    return pl.pallas_call(
        last_kernel,
        in_specs=[pl.BlockSpec(memory_space=pltpu.SMEM)] + vmem(17),
        out_specs=pl.BlockSpec(memory_space=pl.ANY),
        out_shape=jax.ShapeDtypeStruct(shape, BF16),
        scratch_shapes=[
            pltpu.SemaphoreType.DMA,
            pltpu.SemaphoreType.DMA((5,)),
            pltpu.VMEM((rows // ROW, SHIFT_LON, WIN_LEV, d), BF16),
            pltpu.VMEM((2, 2, SHIFT_LAT, SHIFT_LON, WIN_LEV, d), BF16),
        ]
        + layer_scratch(rows + 160, rows // HALF + 4, weights),
        compiler_params=params(),
        cost_estimate=cost(12),
        name="last",
    )(par, near_res, far, far_halo, *edges, *bias, *masks, *weights)


def per_device(tokens, group_ids, bias_table, w_qkv, w_proj, gain_attn, w_in, w_out, gain_mlp):
    samples, lev, lat_rows, lon_cols, d = tokens.shape
    lon_count = lax.axis_size("lon")
    lat_count = lax.axis_size("lat")
    lon_at = lax.axis_index("lon").astype(jnp.int32)
    lat_at = lax.axis_index("lat").astype(jnp.int32)
    par = lax.rem(lon_at, 2)
    near_pairs = [(i, i ^ 1) for i in range(lon_count)]
    far_pairs = [(i, (i + (1 if i % 2 else -1)) % lon_count) for i in range(lon_count)]
    down_pairs = [(i, (i + 1) % lat_count) for i in range(lat_count)]
    up_pairs = [(i, (i - 1) % lat_count) for i in range(lat_count)]
    at = jnp.stack([par, lat_at, lon_at])
    wins = lat_rows // WIN_LAT + 1

    cells = jnp.transpose(tokens[0], (1, 2, 0, 3)).reshape(lat_rows, 2, SHIFT_LON, lev, d)
    near, far, top, bot = pack(at, cells)
    far_halo = lax.ppermute(far, "lon", far_pairs)
    near_halo = lax.ppermute(near, "lon", near_pairs)
    above = lax.ppermute(bot, "lat", down_pairs)
    below = lax.ppermute(top, "lat", up_pairs)
    bias_near, bias_far, mask_near, mask_far, mask_edge = prep(at, group_ids, bias_table.T, wins)
    above, below, bias_near = lax.optimization_barrier((above, below, bias_near))
    edge_near, edge_far = edge_pack(above, top, bot, below)
    edge_near_halo = lax.ppermute(edge_near, "lon", near_pairs)
    edge_far_halo = lax.ppermute(edge_far, "lon", far_pairs)
    weights = [w_qkv, w_proj, w_in, w_out, gain_attn.reshape(1, -1), gain_mlp.reshape(1, -1)]
    near, edge_near = lax.optimization_barrier((near, edge_near))
    near_res = near_layer(near, near_halo, bias_near, mask_near, weights)
    out = last_layer(
        at,
        near_res,
        far,
        far_halo,
        [edge_near, edge_near_halo, edge_far, edge_far_halo],
        [bias_near, bias_far],
        [mask_far, mask_edge],
        weights,
    )
    return jnp.transpose(out.reshape(lat_rows, lon_cols, lev, d), (2, 0, 1, 3))[None]


def solution(mesh):
    in_specs = (P(None, None, "lat", "lon", None), P(), P(), P(), P(), P(), P(), P(), P())
    out_specs = P(None, None, "lat", "lon", None)
    return jax.shard_map(
        per_device, mesh=mesh, in_specs=in_specs, out_specs=out_specs, check_vma=False
    )
```

```python
import functools

import jax
import jax.numpy as jnp
from jax import lax
from jax.experimental import pallas as pl
from jax.experimental.pallas import tpu as pltpu
from jax.sharding import PartitionSpec as P

WIN_LEV = 2
WIN_LAT = 6
WIN_LON = 12
SHIFT_LAT = 3
SHIFT_LON = 6

EPS = 1e-05
LOG2E = 1.4426950408889634
HALF = WIN_LEV * WIN_LAT * SHIFT_LON
ROW = WIN_LEV * SHIFT_LON
EDGE = SHIFT_LAT * ROW
KEYS = 2 * HALF
SPREAD = 256
GROUP = 4
FF_CHUNK = 1024
PREP_US = 2
NEAR_US = 1
VMEM_LIMIT = 24 * 1024 * 1024
PACK_LIMIT = 20 * 1024 * 1024

F32 = jnp.float32
BF16 = jnp.bfloat16


def params(limit=VMEM_LIMIT):
    return pltpu.CompilerParams(vmem_limit_bytes=limit)


def cost(micros):
    return pl.CostEstimate(flops=int(micros * 1e9), bytes_accessed=int(micros * 3e6), transcendentals=0)


def vmem(count):
    return [pl.BlockSpec(memory_space=pltpu.VMEM)] * count


def pack_kernel(par_ref, tok_ref, near_ref, far_ref, top_ref, bot_ref):
    lat, d = tok_ref.shape[0], tok_ref.shape[-1]
    par = par_ref[0]
    for side, out in ((1, far_ref), (0, near_ref)):
        half = par if side else 1 - par
        out[...] = tok_ref[SHIFT_LAT : lat - SHIFT_LAT, half].reshape(out.shape)
        top_ref[side] = tok_ref[:SHIFT_LAT, half].reshape(EDGE, d)
        bot_ref[side] = tok_ref[lat - SHIFT_LAT :, half].reshape(EDGE, d)


def pack(par, cells):
    lat, _, lon, lev, d = cells.shape
    main = (lat - 2 * SHIFT_LAT) * ROW
    return pl.pallas_call(
        pack_kernel,
        in_specs=[pl.BlockSpec(memory_space=pltpu.SMEM)] + vmem(1),
        out_specs=vmem(4),
        out_shape=[
            jax.ShapeDtypeStruct((main, d), BF16),
            jax.ShapeDtypeStruct((main, d), BF16),
            jax.ShapeDtypeStruct((2, EDGE, d), BF16),
            jax.ShapeDtypeStruct((2, EDGE, d), BF16),
        ],
        compiler_params=params(PACK_LIMIT),
        cost_estimate=cost(1),
        name="pack",
    )(par, cells)


def edge_pack_kernel(above_ref, top_ref, bot_ref, below_ref, near_ref, far_ref, scr):
    for side, out in enumerate((near_ref, far_ref)):
        for i, ref in enumerate((above_ref, top_ref, bot_ref, below_ref)):
            scr[i * EDGE : (i + 1) * EDGE, :] = ref[side].astype(F32)
        out[...] = scr[...].astype(BF16)


def edge_pack(above, top, bot, below):
    d = top.shape[2]
    return pl.pallas_call(
        edge_pack_kernel,
        in_specs=vmem(4),
        out_specs=vmem(2),
        out_shape=[jax.ShapeDtypeStruct((4 * EDGE, d), BF16)] * 2,
        scratch_shapes=[pltpu.VMEM((4 * EDGE, d), F32)],
        compiler_params=params(),
        name="edge_pack",
    )(above, top, bot, below)


def prep_kernel(
    at_ref, gid_ref, table_ref, bias_near, bias_far, mask_near, mask_far, mask_edge, wide, kinds
):
    heads, offsets = table_ref.shape
    nw, nh = 2 * WIN_LON - 1, 2 * WIN_LAT - 1
    par, lat_at, lon_at = at_ref[0], at_ref[1], at_ref[2]
    count = wide.shape[1]
    wide[...] = jnp.zeros_like(wide)
    wide[:, :offsets] = table_ref[...] * LOG2E
    x = jnp.broadcast_to(wide[...][:, None, :], (heads, 16, count)).reshape(heads * 16, count)
    place = lax.broadcasted_iota(jnp.int32, x.shape, 0) % 16
    for amount, bit in ((nh * nw, place % 2), (1, place // 2 % 2), (2, place // 4 % 2), (4, place // 8)):
        x = jnp.where(bit == 1, pltpu.roll(x, count - amount, 1), x)
    high = x.astype(BF16)
    low = (x - high.astype(F32)).astype(BF16)
    lane = lax.broadcasted_iota(jnp.int32, (1, SPREAD), 1)
    j, w, z = lane // ROW, lane % ROW // WIN_LEV, lane % WIN_LEV
    source = (WIN_LEV - 1 - z) * nh * nw + (nh - 1 - j) * nw - w
    source = jnp.where(j < nh, source, -count)
    offset = lax.broadcasted_iota(jnp.int32, (count, SPREAD), 0)
    for kind, centre in enumerate((WIN_LON - 1, SHIFT_LON - 1, WIN_LON + SHIFT_LON - 1)):
        m = jnp.where(offset == source + centre, 1.0, 0.0).astype(BF16)
        y = jnp.dot(high, m, preferred_element_type=F32) + jnp.dot(low, m, preferred_element_type=F32)
        kinds[kind] = y.reshape(heads, 16, SPREAD)
    for side, out in enumerate((bias_near, bias_far)):
        halo = kinds[2 - par if side else 1 + par]
        for h in range(WIN_LAT):
            start = (WIN_LAT - 1 - h) * ROW
            out[:, h * ROW : (h + 1) * ROW, :HALF] = kinds[0, :, :ROW, start : start + HALF]
            out[:, h * ROW : (h + 1) * ROW, HALF:KEYS] = halo[:, :ROW, start : start + HALF]
    total, around = gid_ref.shape
    wins = mask_near.shape[0] + 2
    lat_rows = (wins - 1) * WIN_LAT
    lane = lax.broadcasted_iota(jnp.int32, (1, KEYS), 1)
    is_halo = lane >= HALF
    rest = jnp.where(is_halo, lane - HALF, lane)
    h_of = rest // ROW
    w_of = rest % ROW // WIN_LEV
    ids = gid_ref[...].astype(BF16)
    row = lax.broadcasted_iota(jnp.int32, (total, KEYS), 0)
    col = lax.broadcasted_iota(jnp.int32, (around, KEYS), 0)
    for side in range(2):
        right = par == side
        offset = jnp.where(
            right, jnp.where(is_halo, SHIFT_LON, 0), jnp.where(is_halo, -WIN_LON, -SHIFT_LON)
        )
        want = lon_at * 2 * SHIFT_LON + offset + w_of
        want = jnp.where(want < 0, want + around, want)
        pick = jnp.where(col == want, 1.0, 0.0).astype(BF16)
        label = 2.0 * jnp.dot(ids, pick, preferred_element_type=F32)
        label = label + jnp.where(row >= total - SHIFT_LAT, 1.0, 0.0)
        lines = []
        for k in range(wins):
            want = lat_at * lat_rows + (k - 1) * WIN_LAT + h_of
            want = jnp.where(want < 0, want + total, want)
            line = jnp.sum(jnp.where(row == want, label, 0.0), 0, keepdims=True)
            lines.append(line)
        lines = jnp.concatenate(lines, 0)
        cols = lines[:, :128].T
        for k in range(wins):
            same = cols[:HALF, k : k + 1] == lines[k : k + 1, :]
            mask = jnp.where(same, 0.0, -jnp.inf)
            if k == 0:
                mask_edge[2 * side] = mask
            elif k == wins - 1:
                mask_edge[2 * side + 1] = mask
            elif side == 0:
                mask_near[k - 1] = mask
            else:
                mask_far[k - 1] = mask


def prep(at, group_ids, table, wins):
    heads, offsets = table.shape
    count = -(-offsets // 256) * 256
    return pl.pallas_call(
        prep_kernel,
        in_specs=[pl.BlockSpec(memory_space=pltpu.SMEM)] + vmem(2),
        out_specs=vmem(5),
        out_shape=[jax.ShapeDtypeStruct((heads, HALF, KEYS), F32)] * 2
        + [jax.ShapeDtypeStruct((wins - 2, HALF, KEYS), F32)] * 2
        + [jax.ShapeDtypeStruct((4, HALF, KEYS), F32)],
        scratch_shapes=[
            pltpu.VMEM((heads, count), F32),
            pltpu.VMEM((3, heads, 16, SPREAD), F32),
        ],
        compiler_params=params(),
        cost_estimate=cost(PREP_US),
        name="prep",
    )(at, group_ids, table)


def norm_rows(value, gain):
    mean = jnp.mean(value, -1, keepdims=True)
    centred = value - mean
    var = jnp.mean(centred * centred, -1, keepdims=True)
    return centred * lax.rsqrt(var + EPS) * gain


def gelu(x):
    return 0.5 * x * (1.0 + lax.erf(x * 0.7071067811865476))


def attend(q, k, v, extra, mask, lane_head, hd):
    per, lanes = q.shape
    lhs = jnp.concatenate([jnp.where(lane_head == j, q, 0.0) for j in range(GROUP)], 0).astype(BF16)
    sc = lax.dot_general(lhs, k, (((1,), (1,)), ((), ())), preferred_element_type=F32)
    sc = sc + extra.reshape(GROUP * per, KEYS) + mask
    top = jnp.max(sc, -1, keepdims=True)
    p = jnp.exp2(sc - top).astype(BF16)
    v = jnp.concatenate([v, jnp.ones(v.shape, BF16)], 1)
    o = jnp.dot(p, v, preferred_element_type=F32)
    num, den = o[:per, :lanes], o[:per, lanes:]
    for j in range(1, GROUP):
        here = lane_head == j
        num = jnp.where(here, o[j * per : (j + 1) * per, :lanes], num)
        den = jnp.where(here, o[j * per : (j + 1) * per, lanes:], den)
    return num / den


def layer_body(blocks, weights, scratch):
    w_qkv, w_proj, w_in, w_out, gain_attn, gain_mlp = weights
    q_scr, k_scr, v_scr, o_scr, mid_scr, acc_scr = scratch
    d = w_proj.shape[0]
    heads = blocks[0][2].shape[0]
    hd = d // heads
    lanes = GROUP * hd
    groups = heads // GROUP
    scale = LOG2E / hd**0.5
    step = 2 * lanes
    wi = 0
    base = 0
    for own, halo, bias, mask_ref, mask_at, q_lo, q_rows in blocks:
        wins = own.shape[0] // HALF
        per = q_rows // wins
        for c in range(0, d, step):
            q = jnp.dot(own[q_lo : q_lo + q_rows, :], w_qkv[:, c : c + step], preferred_element_type=F32)
            q_scr[base : base + q_rows, c : c + step] = q * scale
            for part in (d, 2 * d):
                w = w_qkv[:, part + c : part + c + step]
                a = jnp.dot(own[...], w, preferred_element_type=F32)
                b = jnp.dot(halo[...], w, preferred_element_type=F32)
                for i in range(wins):
                    both = jnp.concatenate(
                        [a[i * HALF : (i + 1) * HALF], b[i * HALF : (i + 1) * HALF]], 0
                    ).astype(BF16)
                    if part == d:
                        k_scr[wi + i, :, c : c + step] = both
                    else:
                        v_scr[wi + i, :, c : c + step] = both
        lane_head = lax.broadcasted_iota(jnp.int32, (per, lanes), 1) // hd
        for i in range(wins):
            first = q_lo + i * per - i * HALF
            at = base + i * per
            mask = jnp.concatenate([mask_ref[mask_at + i, first : first + per, :]] * GROUP, 0)
            for g in range(groups):
                o_scr[at : at + per, g * lanes : (g + 1) * lanes] = attend(
                    q_scr[at : at + per, g * lanes : (g + 1) * lanes],
                    k_scr[wi + i, :, g * lanes : (g + 1) * lanes],
                    v_scr[wi + i, :, g * lanes : (g + 1) * lanes],
                    bias[g * GROUP : (g + 1) * GROUP, first : first + per, :],
                    mask,
                    lane_head,
                    hd,
                )
        base += q_rows
        wi += wins
    proj = jnp.dot(o_scr[...].astype(BF16), w_proj[...], preferred_element_type=F32)
    branch = norm_rows(proj, gain_attn[...]).astype(BF16).astype(F32)
    base = 0
    for own, _, _, _, _, q_lo, q_rows in blocks:
        mid_scr[base : base + q_rows, :] = (
            own[q_lo : q_lo + q_rows, :].astype(F32) + branch[base : base + q_rows]
        ).astype(BF16)
        base += q_rows
    ff = w_in.shape[1]
    chunk = FF_CHUNK
    for c in range(0, ff, chunk):
        up = jnp.dot(mid_scr[...], w_in[:, c : c + chunk], preferred_element_type=F32)
        hid = gelu(up).astype(BF16)
        down = jnp.dot(hid, w_out[c : c + chunk, :], preferred_element_type=F32)
        if c == 0:
            acc_scr[...] = down
        else:
            acc_scr[...] += down
    return mid_scr[...].astype(F32) + norm_rows(acc_scr[...], gain_mlp[...])


def near_kernel(own, halo, bias, mask, *refs):
    weights, out, scratch = refs[:6], refs[6], refs[7:]
    rows, d = own.shape
    res = layer_body([(own, halo, bias, mask, 0, 0, rows)], weights, scratch)
    out[...] = res.astype(BF16).reshape(out.shape)


def last_kernel(
    par_ref, near_res, far, far_halo, e_near, e_near_halo, e_far, e_far_halo, *refs
):
    bias_near, bias_far, mask_far, mask_edge = refs[:4]
    weights, out, near_sem, sems, far_buf, edge_buf = refs[4:10], *refs[10:15]
    scratch = refs[15:]
    par = par_ref[0]
    lat = out.shape[0]
    halves = (1 - par, par)
    main = pl.ds(SHIFT_LAT, lat - 2 * SHIFT_LAT)
    first = pltpu.make_async_copy(near_res, out.at[main, halves[0]], near_sem)
    first.start()
    rows = far.shape[0]
    lo, keep = EDGE // 8 * 8, 80
    res = layer_body(
        [
            (far, far_halo, bias_far, mask_far, 0, 0, rows),
            (e_near, e_near_halo, bias_near, mask_edge, 0, lo, keep),
            (e_far, e_far_halo, bias_far, mask_edge, 2, lo, keep),
        ],
        weights,
        scratch,
    )
    far_buf[...] = res[:rows].astype(BF16).reshape(far_buf.shape)
    copies = [pltpu.make_async_copy(far_buf, out.at[main, halves[1]], sems.at[4])]
    copies[0].start()
    shape = edge_buf.shape[2:]
    for side in range(2):
        at = rows + side * keep + EDGE - lo
        for end in range(2):
            part = res[at + end * EDGE : at + (end + 1) * EDGE]
            edge_buf[side, end] = part.reshape(shape).astype(BF16)
            place = pl.ds(end * (lat - SHIFT_LAT), SHIFT_LAT)
            copies.append(
                pltpu.make_async_copy(
                    edge_buf.at[side, end], out.at[place, halves[side]], sems.at[2 * side + end]
                )
            )
            copies[-1].start()
    for copy in copies:
        copy.wait()
    first.wait()


def layer_scratch(total, windows, weights):
    d = weights[1].shape[0]
    return [
        pltpu.VMEM((total, d), F32),
        pltpu.VMEM((windows, KEYS, d), BF16),
        pltpu.VMEM((windows, KEYS, d), BF16),
        pltpu.VMEM((total, d), F32),
        pltpu.VMEM((total, d), BF16),
        pltpu.VMEM((total, d), F32),
    ]


def near_layer(own, halo, bias, mask, weights):
    rows, d = own.shape
    shape = (rows // ROW, SHIFT_LON, WIN_LEV, d)
    return pl.pallas_call(
        near_kernel,
        in_specs=vmem(10),
        out_specs=vmem(1)[0],
        out_shape=jax.ShapeDtypeStruct(shape, BF16),
        scratch_shapes=layer_scratch(rows, rows // HALF, weights),
        compiler_params=params(),
        cost_estimate=cost(NEAR_US),
        name="near",
    )(own, halo, bias, mask, *weights)


def last_layer(par, near_res, far, far_halo, edges, bias, masks, weights):
    rows, d = far.shape
    lat = rows // ROW + 2 * SHIFT_LAT
    shape = (lat, 2, SHIFT_LON, WIN_LEV, d)
    return pl.pallas_call(
        last_kernel,
        in_specs=[pl.BlockSpec(memory_space=pltpu.SMEM)] + vmem(17),
        out_specs=pl.BlockSpec(memory_space=pl.ANY),
        out_shape=jax.ShapeDtypeStruct(shape, BF16),
        scratch_shapes=[
            pltpu.SemaphoreType.DMA,
            pltpu.SemaphoreType.DMA((5,)),
            pltpu.VMEM((rows // ROW, SHIFT_LON, WIN_LEV, d), BF16),
            pltpu.VMEM((2, 2, SHIFT_LAT, SHIFT_LON, WIN_LEV, d), BF16),
        ]
        + layer_scratch(rows + 160, rows // HALF + 4, weights),
        compiler_params=params(),
        cost_estimate=cost(12),
        name="last",
    )(par, near_res, far, far_halo, *edges, *bias, *masks, *weights)


def per_device(tokens, group_ids, bias_table, w_qkv, w_proj, gain_attn, w_in, w_out, gain_mlp):
    samples, lev, lat_rows, lon_cols, d = tokens.shape
    lon_count = lax.axis_size("lon")
    lat_count = lax.axis_size("lat")
    lon_at = lax.axis_index("lon").astype(jnp.int32)
    lat_at = lax.axis_index("lat").astype(jnp.int32)
    par = lax.rem(lon_at, 2)
    near_pairs = [(i, i ^ 1) for i in range(lon_count)]
    far_pairs = [(i, (i + (1 if i % 2 else -1)) % lon_count) for i in range(lon_count)]
    down_pairs = [(i, (i + 1) % lat_count) for i in range(lat_count)]
    up_pairs = [(i, (i - 1) % lat_count) for i in range(lat_count)]
    at = jnp.stack([par, lat_at, lon_at])
    wins = lat_rows // WIN_LAT + 1

    cells = jnp.transpose(tokens[0], (1, 2, 0, 3)).reshape(lat_rows, 2, SHIFT_LON, lev, d)
    near, far, top, bot = pack(at, cells)
    far_halo = lax.ppermute(far, "lon", far_pairs)
    near_halo = lax.ppermute(near, "lon", near_pairs)
    above = lax.ppermute(bot, "lat", down_pairs)
    below = lax.ppermute(top, "lat", up_pairs)
    bias_near, bias_far, mask_near, mask_far, mask_edge = prep(at, group_ids, bias_table.T, wins)
    above, below, bias_near = lax.optimization_barrier((above, below, bias_near))
    edge_near, edge_far = edge_pack(above, top, bot, below)
    edge_near_halo = lax.ppermute(edge_near, "lon", near_pairs)
    edge_far_halo = lax.ppermute(edge_far, "lon", far_pairs)
    weights = [w_qkv, w_proj, w_in, w_out, gain_attn.reshape(1, -1), gain_mlp.reshape(1, -1)]
    near, edge_near = lax.optimization_barrier((near, edge_near))
    near_res = near_layer(near, near_halo, bias_near, mask_near, weights)
    out = last_layer(
        at,
        near_res,
        far,
        far_halo,
        [edge_near, edge_near_halo, edge_far, edge_far_halo],
        [bias_near, bias_far],
        [mask_far, mask_edge],
        weights,
    )
    return jnp.transpose(out.reshape(lat_rows, lon_cols, lev, d), (2, 0, 1, 3))[None]


def solution(mesh):
    in_specs = (P(None, None, "lat", "lon", None), P(), P(), P(), P(), P(), P(), P(), P())
    out_specs = P(None, None, "lat", "lon", None)
    return jax.shard_map(
        per_device, mesh=mesh, in_specs=in_specs, out_specs=out_specs, check_vma=False
    )
```

```python
import functools

import jax
import jax.numpy as jnp
from jax import lax
from jax.experimental import pallas as pl
from jax.experimental.pallas import tpu as pltpu
from jax.sharding import PartitionSpec as P

WIN_LEV = 2
WIN_LAT = 6
WIN_LON = 12
SHIFT_LAT = 3
SHIFT_LON = 6

EPS = 1e-05
LOG2E = 1.4426950408889634
HALF = WIN_LEV * WIN_LAT * SHIFT_LON
ROW = WIN_LEV * SHIFT_LON
EDGE = SHIFT_LAT * ROW
KEYS = 2 * HALF
SPREAD = 256
GROUP = 4
FF_CHUNK = 1024
PREP_US = 2
NEAR_US = 1
VMEM_LIMIT = 24 * 1024 * 1024
PACK_LIMIT = 20 * 1024 * 1024

F32 = jnp.float32
BF16 = jnp.bfloat16


def params(limit=VMEM_LIMIT):
    return pltpu.CompilerParams(vmem_limit_bytes=limit)


def cost(micros):
    return pl.CostEstimate(flops=int(micros * 1e9), bytes_accessed=int(micros * 3e6), transcendentals=0)


def vmem(count):
    return [pl.BlockSpec(memory_space=pltpu.VMEM)] * count


def pack_kernel(par_ref, tok_ref, near_ref, far_ref, top_ref, bot_ref):
    lat, d = tok_ref.shape[0], tok_ref.shape[-1]
    par = par_ref[0]
    for side, out in ((1, far_ref), (0, near_ref)):
        half = par if side else 1 - par
        out[...] = tok_ref[SHIFT_LAT : lat - SHIFT_LAT, half].reshape(out.shape)
        top_ref[side] = tok_ref[:SHIFT_LAT, half].reshape(EDGE, d)
        bot_ref[side] = tok_ref[lat - SHIFT_LAT :, half].reshape(EDGE, d)


def pack(par, cells):
    lat, _, lon, lev, d = cells.shape
    main = (lat - 2 * SHIFT_LAT) * ROW
    return pl.pallas_call(
        pack_kernel,
        in_specs=[pl.BlockSpec(memory_space=pltpu.SMEM)] + vmem(1),
        out_specs=vmem(4),
        out_shape=[
            jax.ShapeDtypeStruct((main, d), BF16),
            jax.ShapeDtypeStruct((main, d), BF16),
            jax.ShapeDtypeStruct((2, EDGE, d), BF16),
            jax.ShapeDtypeStruct((2, EDGE, d), BF16),
        ],
        compiler_params=params(PACK_LIMIT),
        cost_estimate=cost(1),
        name="pack",
    )(par, cells)


def edge_pack_kernel(above_ref, top_ref, bot_ref, below_ref, near_ref, far_ref, scr):
    for side, out in enumerate((near_ref, far_ref)):
        for i, ref in enumerate((above_ref, top_ref, bot_ref, below_ref)):
            scr[i * EDGE : (i + 1) * EDGE, :] = ref[side].astype(F32)
        out[...] = scr[...].astype(BF16)


def edge_pack(above, top, bot, below):
    d = top.shape[2]
    return pl.pallas_call(
        edge_pack_kernel,
        in_specs=vmem(4),
        out_specs=vmem(2),
        out_shape=[jax.ShapeDtypeStruct((4 * EDGE, d), BF16)] * 2,
        scratch_shapes=[pltpu.VMEM((4 * EDGE, d), F32)],
        compiler_params=params(),
        name="edge_pack",
    )(above, top, bot, below)


def prep_kernel(
    at_ref, gid_ref, table_ref, bias_near, bias_far, mask_near, mask_far, mask_edge, wide, kinds
):
    heads, offsets = table_ref.shape
    nw, nh = 2 * WIN_LON - 1, 2 * WIN_LAT - 1
    par, lat_at, lon_at = at_ref[0], at_ref[1], at_ref[2]
    count = wide.shape[1]
    wide[...] = jnp.zeros_like(wide)
    wide[:, :offsets] = table_ref[...] * LOG2E
    rows = (heads, 16, count)
    first = jnp.broadcast_to(wide[...][:, None, :], rows).reshape(heads * 16, count)
    later = pltpu.roll(wide[...], count - nh * nw, 1)
    later = jnp.broadcast_to(later[:, None, :], rows).reshape(heads * 16, count)
    place = lax.broadcasted_iota(jnp.int32, first.shape, 0) % 16
    x = jnp.where(place % 2 == 1, later, first)
    for amount, bit in ((1, place // 2 % 2), (2, place // 4 % 2), (4, place // 8)):
        x = jnp.where(bit == 1, pltpu.roll(x, count - amount, 1), x)
    high = x.astype(BF16)
    low = (x - high.astype(F32)).astype(BF16)
    lane = lax.broadcasted_iota(jnp.int32, (1, SPREAD), 1)
    j, w, z = lane // ROW, lane % ROW // WIN_LEV, lane % WIN_LEV
    source = (WIN_LEV - 1 - z) * nh * nw + (nh - 1 - j) * nw - w
    ahead = source + WIN_LAT * nw
    source = jnp.where(j < nh, source, -count)
    ahead = jnp.where((j >= WIN_LAT) & (j < nh + WIN_LAT), ahead, -count)
    offset = lax.broadcasted_iota(jnp.int32, (count, SPREAD), 0)
    for kind, centre in enumerate((WIN_LON - 1, SHIFT_LON - 1, WIN_LON + SHIFT_LON - 1)):
        m = jnp.where(offset == (ahead if kind else source) + centre, 1.0, 0.0).astype(BF16)
        y = jnp.dot(high, m, preferred_element_type=F32) + jnp.dot(low, m, preferred_element_type=F32)
        kinds[kind] = y
    for side, out in enumerate((bias_near, bias_far)):
        halo = kinds[2 - par if side else 1 + par]
        for h in range(WIN_LAT):
            start = (WIN_LAT - 1 - h) * ROW
            both = jnp.where(lane < HALF + start, kinds[0], halo)
            if start:
                both = pltpu.roll(both, SPREAD - start, 1)
            both = both.reshape(heads, 16, SPREAD)
            out[:, h * ROW : (h + 1) * ROW, :] = both[:, :ROW, :KEYS]
    total, around = gid_ref.shape
    wins = mask_near.shape[0] + 2
    lat_rows = (wins - 1) * WIN_LAT
    lane = lax.broadcasted_iota(jnp.int32, (1, KEYS), 1)
    is_halo = lane >= HALF
    rest = jnp.where(is_halo, lane - HALF, lane)
    h_of = rest // ROW
    w_of = rest % ROW // WIN_LEV
    span = wins * WIN_LAT
    place = lat_at * lat_rows - WIN_LAT + lax.broadcasted_iota(jnp.int32, (span, 1), 0)
    place = jnp.where(place < 0, place + total, place)
    pick = jnp.where(lax.broadcasted_iota(jnp.int32, (span, total), 1) == place, 1.0, 0.0)
    ids = jnp.dot(pick.astype(BF16), gid_ref[...].astype(BF16), preferred_element_type=F32).astype(BF16)
    region = jnp.where(place >= total - SHIFT_LAT, 1.0, 0.0)
    row = lax.broadcasted_iota(jnp.int32, (span, KEYS), 0)
    window = lax.broadcasted_iota(jnp.int32, (wins, span), 0)
    inside = lax.broadcasted_iota(jnp.int32, (wins, span), 1) // WIN_LAT
    gather = jnp.where(window == inside, 1.0, 0.0).astype(BF16)
    col = lax.broadcasted_iota(jnp.int32, (around, KEYS), 0)
    for side in range(2):
        right = par == side
        offset = jnp.where(
            right, jnp.where(is_halo, SHIFT_LON, 0), jnp.where(is_halo, -WIN_LON, -SHIFT_LON)
        )
        want = lon_at * 2 * SHIFT_LON + offset + w_of
        want = jnp.where(want < 0, want + around, want)
        pick = jnp.where(col == want, 1.0, 0.0).astype(BF16)
        label = 2.0 * jnp.dot(ids, pick, preferred_element_type=F32)
        label = jnp.where(row % WIN_LAT == h_of, label + region, 0.0).astype(BF16)
        lines = jnp.dot(gather, label, preferred_element_type=F32)
        cols = lines[:, :128].T
        for k in range(wins):
            same = cols[:HALF, k : k + 1] == lines[k : k + 1, :]
            mask = jnp.where(same, 0.0, -jnp.inf)
            if k == 0:
                mask_edge[2 * side] = mask
            elif k == wins - 1:
                mask_edge[2 * side + 1] = mask
            elif side == 0:
                mask_near[k - 1] = mask
            else:
                mask_far[k - 1] = mask


def prep(at, group_ids, table, wins):
    heads, offsets = table.shape
    count = -(-offsets // 256) * 256
    return pl.pallas_call(
        prep_kernel,
        in_specs=[pl.BlockSpec(memory_space=pltpu.SMEM)] + vmem(2),
        out_specs=vmem(5),
        out_shape=[jax.ShapeDtypeStruct((heads, HALF, KEYS), F32)] * 2
        + [jax.ShapeDtypeStruct((wins - 2, HALF, KEYS), F32)] * 2
        + [jax.ShapeDtypeStruct((4, HALF, KEYS), F32)],
        scratch_shapes=[
            pltpu.VMEM((heads, count), F32),
            pltpu.VMEM((3, heads * 16, SPREAD), F32),
        ],
        compiler_params=params(),
        cost_estimate=cost(PREP_US),
        name="prep",
    )(at, group_ids, table)


def norm_rows(value, gain):
    mean = jnp.mean(value, -1, keepdims=True)
    centred = value - mean
    var = jnp.mean(centred * centred, -1, keepdims=True)
    return centred * lax.rsqrt(var + EPS) * gain


def gelu(x):
    return 0.5 * x * (1.0 + lax.erf(x * 0.7071067811865476))


def attend(q, k, v, extra, mask, lane_head, hd):
    per, lanes = q.shape
    lhs = jnp.concatenate([jnp.where(lane_head == j, q, 0.0) for j in range(GROUP)], 0).astype(BF16)
    sc = lax.dot_general(lhs, k, (((1,), (1,)), ((), ())), preferred_element_type=F32)
    sc = sc + extra.reshape(GROUP * per, KEYS) + mask
    top = jnp.max(sc, -1, keepdims=True)
    p = jnp.exp2(sc - top).astype(BF16)
    v = jnp.concatenate([v, jnp.ones(v.shape, BF16)], 1)
    o = jnp.dot(p, v, preferred_element_type=F32)
    num, den = o[:per, :lanes], o[:per, lanes:]
    for j in range(1, GROUP):
        here = lane_head == j
        num = jnp.where(here, o[j * per : (j + 1) * per, :lanes], num)
        den = jnp.where(here, o[j * per : (j + 1) * per, lanes:], den)
    return num / den


def layer_body(blocks, weights, scratch):
    w_qkv, w_proj, w_in, w_out, gain_attn, gain_mlp = weights
    q_scr, k_scr, v_scr, o_scr, mid_scr, acc_scr = scratch
    d = w_proj.shape[0]
    heads = blocks[0][2].shape[0]
    hd = d // heads
    lanes = GROUP * hd
    groups = heads // GROUP
    scale = LOG2E / hd**0.5
    step = 2 * lanes
    asking = jnp.concatenate([own[q_lo : q_lo + n, :] for own, _, _, _, _, q_lo, n in blocks], 0)
    rows = jnp.concatenate([ref[...] for own, halo, *_ in blocks for ref in (own, halo)], 0)
    for c in range(0, d, step):
        q = jnp.dot(asking, w_qkv[:, c : c + step], preferred_element_type=F32)
        q_scr[:, c : c + step] = q * scale
        for part, scr in ((d, k_scr), (2 * d, v_scr)):
            y = jnp.dot(rows, w_qkv[:, part + c : part + c + step], preferred_element_type=F32)
            at = 0
            wi = 0
            for own, halo, *_ in blocks:
                size = own.shape[0]
                for i in range(size // HALF):
                    a = y[at + i * HALF : at + (i + 1) * HALF]
                    b = y[at + size + i * HALF : at + size + (i + 1) * HALF]
                    scr[wi, :, c : c + step] = jnp.concatenate([a, b], 0).astype(BF16)
                    wi += 1
                at += 2 * size
    base = 0
    wi = 0
    for own, halo, bias, mask_ref, mask_at, q_lo, q_rows in blocks:
        wins = own.shape[0] // HALF
        per = q_rows // wins
        lane_head = lax.broadcasted_iota(jnp.int32, (per, lanes), 1) // hd
        for i in range(wins):
            first = q_lo + i * per - i * HALF
            at = base + i * per
            mask = jnp.concatenate([mask_ref[mask_at + i, first : first + per, :]] * GROUP, 0)
            for g in range(groups):
                o_scr[at : at + per, g * lanes : (g + 1) * lanes] = attend(
                    q_scr[at : at + per, g * lanes : (g + 1) * lanes],
                    k_scr[wi + i, :, g * lanes : (g + 1) * lanes],
                    v_scr[wi + i, :, g * lanes : (g + 1) * lanes],
                    bias[g * GROUP : (g + 1) * GROUP, first : first + per, :],
                    mask,
                    lane_head,
                    hd,
                )
        base += q_rows
        wi += wins
    proj = jnp.dot(o_scr[...].astype(BF16), w_proj[...], preferred_element_type=F32)
    branch = norm_rows(proj, gain_attn[...]).astype(BF16).astype(F32)
    base = 0
    for own, _, _, _, _, q_lo, q_rows in blocks:
        mid_scr[base : base + q_rows, :] = (
            own[q_lo : q_lo + q_rows, :].astype(F32) + branch[base : base + q_rows]
        ).astype(BF16)
        base += q_rows
    ff = w_in.shape[1]
    chunk = FF_CHUNK
    for c in range(0, ff, chunk):
        up = jnp.dot(mid_scr[...], w_in[:, c : c + chunk], preferred_element_type=F32)
        hid = gelu(up).astype(BF16)
        down = jnp.dot(hid, w_out[c : c + chunk, :], preferred_element_type=F32)
        if c == 0:
            acc_scr[...] = down
        else:
            acc_scr[...] += down
    return mid_scr[...].astype(F32) + norm_rows(acc_scr[...], gain_mlp[...])


def near_kernel(own, halo, bias, mask, *refs):
    weights, out, scratch = refs[:6], refs[6], refs[7:]
    rows, d = own.shape
    res = layer_body([(own, halo, bias, mask, 0, 0, rows)], weights, scratch)
    out[...] = res.astype(BF16).reshape(out.shape)


def last_kernel(
    par_ref, near_res, far, far_halo, e_near, e_near_halo, e_far, e_far_halo, *refs
):
    bias_near, bias_far, mask_far, mask_edge = refs[:4]
    weights, out, near_sem, sems, far_buf, edge_buf = refs[4:10], *refs[10:15]
    scratch = refs[15:]
    par = par_ref[0]
    lat = out.shape[0]
    halves = (1 - par, par)
    main = pl.ds(SHIFT_LAT, lat - 2 * SHIFT_LAT)
    first = pltpu.make_async_copy(near_res, out.at[main, halves[0]], near_sem)
    first.start()
    rows = far.shape[0]
    lo, keep = EDGE // 8 * 8, 80
    res = layer_body(
        [
            (far, far_halo, bias_far, mask_far, 0, 0, rows),
            (e_near, e_near_halo, bias_near, mask_edge, 0, lo, keep),
            (e_far, e_far_halo, bias_far, mask_edge, 2, lo, keep),
        ],
        weights,
        scratch,
    )
    far_buf[...] = res[:rows].astype(BF16).reshape(far_buf.shape)
    copies = [pltpu.make_async_copy(far_buf, out.at[main, halves[1]], sems.at[4])]
    copies[0].start()
    shape = edge_buf.shape[2:]
    for side in range(2):
        at = rows + side * keep + EDGE - lo
        for end in range(2):
            part = res[at + end * EDGE : at + (end + 1) * EDGE]
            edge_buf[side, end] = part.reshape(shape).astype(BF16)
            place = pl.ds(end * (lat - SHIFT_LAT), SHIFT_LAT)
            copies.append(
                pltpu.make_async_copy(
                    edge_buf.at[side, end], out.at[place, halves[side]], sems.at[2 * side + end]
                )
            )
            copies[-1].start()
    for copy in copies:
        copy.wait()
    first.wait()


def layer_scratch(total, windows, weights):
    d = weights[1].shape[0]
    return [
        pltpu.VMEM((total, d), F32),
        pltpu.VMEM((windows, KEYS, d), BF16),
        pltpu.VMEM((windows, KEYS, d), BF16),
        pltpu.VMEM((total, d), F32),
        pltpu.VMEM((total, d), BF16),
        pltpu.VMEM((total, d), F32),
    ]


def near_layer(own, halo, bias, mask, weights):
    rows, d = own.shape
    shape = (rows // ROW, SHIFT_LON, WIN_LEV, d)
    return pl.pallas_call(
        near_kernel,
        in_specs=vmem(10),
        out_specs=vmem(1)[0],
        out_shape=jax.ShapeDtypeStruct(shape, BF16),
        scratch_shapes=layer_scratch(rows, rows // HALF, weights),
        compiler_params=params(),
        cost_estimate=cost(NEAR_US),
        name="near",
    )(own, halo, bias, mask, *weights)


def last_layer(par, near_res, far, far_halo, edges, bias, masks, weights):
    rows, d = far.shape
    lat = rows // ROW + 2 * SHIFT_LAT
    shape = (lat, 2, SHIFT_LON, WIN_LEV, d)
    return pl.pallas_call(
        last_kernel,
        in_specs=[pl.BlockSpec(memory_space=pltpu.SMEM)] + vmem(17),
        out_specs=pl.BlockSpec(memory_space=pl.ANY),
        out_shape=jax.ShapeDtypeStruct(shape, BF16),
        scratch_shapes=[
            pltpu.SemaphoreType.DMA,
            pltpu.SemaphoreType.DMA((5,)),
            pltpu.VMEM((rows // ROW, SHIFT_LON, WIN_LEV, d), BF16),
            pltpu.VMEM((2, 2, SHIFT_LAT, SHIFT_LON, WIN_LEV, d), BF16),
        ]
        + layer_scratch(rows + 160, rows // HALF + 4, weights),
        compiler_params=params(),
        cost_estimate=cost(12),
        name="last",
    )(par, near_res, far, far_halo, *edges, *bias, *masks, *weights)


def per_device(tokens, group_ids, bias_table, w_qkv, w_proj, gain_attn, w_in, w_out, gain_mlp):
    samples, lev, lat_rows, lon_cols, d = tokens.shape
    lon_count = lax.axis_size("lon")
    lat_count = lax.axis_size("lat")
    lon_at = lax.axis_index("lon").astype(jnp.int32)
    lat_at = lax.axis_index("lat").astype(jnp.int32)
    par = lax.rem(lon_at, 2)
    near_pairs = [(i, i ^ 1) for i in range(lon_count)]
    far_pairs = [(i, (i + (1 if i % 2 else -1)) % lon_count) for i in range(lon_count)]
    down_pairs = [(i, (i + 1) % lat_count) for i in range(lat_count)]
    up_pairs = [(i, (i - 1) % lat_count) for i in range(lat_count)]
    at = jnp.stack([par, lat_at, lon_at])
    wins = lat_rows // WIN_LAT + 1

    cells = jnp.transpose(tokens[0], (1, 2, 0, 3)).reshape(lat_rows, 2, SHIFT_LON, lev, d)
    near, far, top, bot = pack(at, cells)
    far_halo = lax.ppermute(far, "lon", far_pairs)
    near_halo = lax.ppermute(near, "lon", near_pairs)
    above = lax.ppermute(bot, "lat", down_pairs)
    below = lax.ppermute(top, "lat", up_pairs)
    bias_near, bias_far, mask_near, mask_far, mask_edge = prep(at, group_ids, bias_table.T, wins)
    above, below, bias_near = lax.optimization_barrier((above, below, bias_near))
    edge_near, edge_far = edge_pack(above, top, bot, below)
    edge_near_halo = lax.ppermute(edge_near, "lon", near_pairs)
    edge_far_halo = lax.ppermute(edge_far, "lon", far_pairs)
    weights = [w_qkv, w_proj, w_in, w_out, gain_attn.reshape(1, -1), gain_mlp.reshape(1, -1)]
    near, edge_near = lax.optimization_barrier((near, edge_near))
    near_res = near_layer(near, near_halo, bias_near, mask_near, weights)
    out = last_layer(
        at,
        near_res,
        far,
        far_halo,
        [edge_near, edge_near_halo, edge_far, edge_far_halo],
        [bias_near, bias_far],
        [mask_far, mask_edge],
        weights,
    )
    return jnp.transpose(out.reshape(lat_rows, lon_cols, lev, d), (2, 0, 1, 3))[None]


def solution(mesh):
    in_specs = (P(None, None, "lat", "lon", None), P(), P(), P(), P(), P(), P(), P(), P())
    out_specs = P(None, None, "lat", "lon", None)
    return jax.shard_map(
        per_device, mesh=mesh, in_specs=in_specs, out_specs=out_specs, check_vma=False
    )
```

```python
import functools

import jax
import jax.numpy as jnp
from jax import lax
from jax.experimental import pallas as pl
from jax.experimental.pallas import tpu as pltpu
from jax.sharding import PartitionSpec as P

WIN_LEV = 2
WIN_LAT = 6
WIN_LON = 12
SHIFT_LAT = 3
SHIFT_LON = 6

EPS = 1e-05
LOG2E = 1.4426950408889634
HALF = WIN_LEV * WIN_LAT * SHIFT_LON
ROW = WIN_LEV * SHIFT_LON
EDGE = SHIFT_LAT * ROW
KEYS = 2 * HALF
SPREAD = 256
GROUP = 4
FF_CHUNK = 1024
PREP_US = 2
NEAR_US = 1
VMEM_LIMIT = 24 * 1024 * 1024
PACK_LIMIT = 20 * 1024 * 1024

F32 = jnp.float32
BF16 = jnp.bfloat16


def params(limit=VMEM_LIMIT):
    return pltpu.CompilerParams(vmem_limit_bytes=limit)


def cost(micros):
    return pl.CostEstimate(flops=int(micros * 1e9), bytes_accessed=int(micros * 3e6), transcendentals=0)


def vmem(count):
    return [pl.BlockSpec(memory_space=pltpu.VMEM)] * count


def pack_kernel(par_ref, tok_ref, near_ref, far_ref, top_ref, bot_ref):
    lat, d = tok_ref.shape[0], tok_ref.shape[-1]
    par = par_ref[0]
    for side, out in ((1, far_ref), (0, near_ref)):
        half = par if side else 1 - par
        out[...] = tok_ref[SHIFT_LAT : lat - SHIFT_LAT, half].reshape(out.shape)
        top_ref[side] = tok_ref[:SHIFT_LAT, half].reshape(EDGE, d)
        bot_ref[side] = tok_ref[lat - SHIFT_LAT :, half].reshape(EDGE, d)


def pack(par, cells):
    lat, _, lon, lev, d = cells.shape
    main = (lat - 2 * SHIFT_LAT) * ROW
    return pl.pallas_call(
        pack_kernel,
        in_specs=[pl.BlockSpec(memory_space=pltpu.SMEM)] + vmem(1),
        out_specs=vmem(4),
        out_shape=[
            jax.ShapeDtypeStruct((main, d), BF16),
            jax.ShapeDtypeStruct((main, d), BF16),
            jax.ShapeDtypeStruct((2, EDGE, d), BF16),
            jax.ShapeDtypeStruct((2, EDGE, d), BF16),
        ],
        compiler_params=params(PACK_LIMIT),
        cost_estimate=cost(1),
        name="pack",
    )(par, cells)


def edge_pack_kernel(above_ref, top_ref, bot_ref, below_ref, near_ref, far_ref, scr):
    for side, out in enumerate((near_ref, far_ref)):
        for i, ref in enumerate((above_ref, top_ref, bot_ref, below_ref)):
            scr[i * EDGE : (i + 1) * EDGE, :] = ref[side].astype(F32)
        out[...] = scr[...].astype(BF16)


def edge_pack(above, top, bot, below):
    d = top.shape[2]
    return pl.pallas_call(
        edge_pack_kernel,
        in_specs=vmem(4),
        out_specs=vmem(2),
        out_shape=[jax.ShapeDtypeStruct((4 * EDGE, d), BF16)] * 2,
        scratch_shapes=[pltpu.VMEM((4 * EDGE, d), F32)],
        compiler_params=params(),
        name="edge_pack",
    )(above, top, bot, below)


def prep_kernel(
    at_ref,
    gid_ref,
    table_ref,
    near_own,
    near_halo,
    w_qkv,
    bias_near,
    bias_far,
    mask_near,
    mask_far,
    mask_edge,
    q,
    k,
    v,
    wide,
    kinds,
):
    heads, offsets = table_ref.shape
    nw, nh = 2 * WIN_LON - 1, 2 * WIN_LAT - 1
    par, lat_at, lon_at = at_ref[0], at_ref[1], at_ref[2]
    count = wide.shape[1]
    wide[...] = jnp.zeros_like(wide)
    wide[:, :offsets] = table_ref[...] * LOG2E
    rows = (heads, 16, count)
    first = jnp.broadcast_to(wide[...][:, None, :], rows).reshape(heads * 16, count)
    later = pltpu.roll(wide[...], count - nh * nw, 1)
    later = jnp.broadcast_to(later[:, None, :], rows).reshape(heads * 16, count)
    place = lax.broadcasted_iota(jnp.int32, first.shape, 0) % 16
    x = jnp.where(place % 2 == 1, later, first)
    for amount, bit in ((1, place // 2 % 2), (2, place // 4 % 2), (4, place // 8)):
        x = jnp.where(bit == 1, pltpu.roll(x, count - amount, 1), x)
    high = x.astype(BF16)
    low = (x - high.astype(F32)).astype(BF16)
    lane = lax.broadcasted_iota(jnp.int32, (1, SPREAD), 1)
    j, w, z = lane // ROW, lane % ROW // WIN_LEV, lane % WIN_LEV
    source = (WIN_LEV - 1 - z) * nh * nw + (nh - 1 - j) * nw - w
    ahead = source + WIN_LAT * nw
    source = jnp.where(j < nh, source, -count)
    ahead = jnp.where((j >= WIN_LAT) & (j < nh + WIN_LAT), ahead, -count)
    offset = lax.broadcasted_iota(jnp.int32, (count, SPREAD), 0)
    for kind, centre in enumerate((WIN_LON - 1, SHIFT_LON - 1, WIN_LON + SHIFT_LON - 1)):
        m = jnp.where(offset == (ahead if kind else source) + centre, 1.0, 0.0).astype(BF16)
        y = jnp.dot(high, m, preferred_element_type=F32) + jnp.dot(low, m, preferred_element_type=F32)
        kinds[kind] = y
    for side, out in enumerate((bias_near, bias_far)):
        halo = kinds[2 - par if side else 1 + par]
        for h in range(WIN_LAT):
            start = (WIN_LAT - 1 - h) * ROW
            both = jnp.where(lane < HALF + start, kinds[0], halo)
            if start:
                both = pltpu.roll(both, SPREAD - start, 1)
            both = both.reshape(heads, 16, SPREAD)
            out[:, h * ROW : (h + 1) * ROW, :] = both[:, :ROW, :KEYS]
    scale = LOG2E / (w_qkv.shape[0] // heads) ** 0.5
    project([(near_own, near_halo, None, None, 0, 0, near_own.shape[0])], w_qkv, q, k, v, scale)
    total, around = gid_ref.shape
    wins = mask_near.shape[0] + 2
    lat_rows = (wins - 1) * WIN_LAT
    lane = lax.broadcasted_iota(jnp.int32, (1, KEYS), 1)
    is_halo = lane >= HALF
    rest = jnp.where(is_halo, lane - HALF, lane)
    h_of = rest // ROW
    w_of = rest % ROW // WIN_LEV
    span = wins * WIN_LAT
    place = lat_at * lat_rows - WIN_LAT + lax.broadcasted_iota(jnp.int32, (span, 1), 0)
    place = jnp.where(place < 0, place + total, place)
    pick = jnp.where(lax.broadcasted_iota(jnp.int32, (span, total), 1) == place, 1.0, 0.0)
    ids = jnp.dot(pick.astype(BF16), gid_ref[...].astype(BF16), preferred_element_type=F32).astype(BF16)
    region = jnp.where(place >= total - SHIFT_LAT, 1.0, 0.0)
    row = lax.broadcasted_iota(jnp.int32, (span, KEYS), 0)
    window = lax.broadcasted_iota(jnp.int32, (wins, span), 0)
    inside = lax.broadcasted_iota(jnp.int32, (wins, span), 1) // WIN_LAT
    gather = jnp.where(window == inside, 1.0, 0.0).astype(BF16)
    col = lax.broadcasted_iota(jnp.int32, (around, KEYS), 0)
    for side in range(2):
        right = par == side
        offset = jnp.where(
            right, jnp.where(is_halo, SHIFT_LON, 0), jnp.where(is_halo, -WIN_LON, -SHIFT_LON)
        )
        want = lon_at * 2 * SHIFT_LON + offset + w_of
        want = jnp.where(want < 0, want + around, want)
        pick = jnp.where(col == want, 1.0, 0.0).astype(BF16)
        label = 2.0 * jnp.dot(ids, pick, preferred_element_type=F32)
        label = jnp.where(row % WIN_LAT == h_of, label + region, 0.0).astype(BF16)
        lines = jnp.dot(gather, label, preferred_element_type=F32)
        cols = lines[:, :128].T
        for k in range(wins):
            same = cols[:HALF, k : k + 1] == lines[k : k + 1, :]
            mask = jnp.where(same, 0.0, -jnp.inf)
            if k == 0:
                mask_edge[2 * side] = mask
            elif k == wins - 1:
                mask_edge[2 * side + 1] = mask
            elif side == 0:
                mask_near[k - 1] = mask
            else:
                mask_far[k - 1] = mask


def prep(at, group_ids, table, own, halo, w_qkv, wins):
    rows, d = own.shape
    heads, offsets = table.shape
    count = -(-offsets // 256) * 256
    return pl.pallas_call(
        prep_kernel,
        in_specs=[pl.BlockSpec(memory_space=pltpu.SMEM)] + vmem(5),
        out_specs=vmem(8),
        out_shape=[jax.ShapeDtypeStruct((heads, HALF, KEYS), F32)] * 2
        + [jax.ShapeDtypeStruct((wins - 2, HALF, KEYS), F32)] * 2
        + [jax.ShapeDtypeStruct((4, HALF, KEYS), F32), jax.ShapeDtypeStruct((rows, d), F32)]
        + [jax.ShapeDtypeStruct((rows // HALF, KEYS, d), BF16)] * 2,
        scratch_shapes=[
            pltpu.VMEM((heads, count), F32),
            pltpu.VMEM((3, heads * 16, SPREAD), F32),
        ],
        compiler_params=params(),
        cost_estimate=cost(PREP_US),
        name="prep",
    )(at, group_ids, table, own, halo, w_qkv)


def norm_rows(value, gain):
    mean = jnp.mean(value, -1, keepdims=True)
    centred = value - mean
    var = jnp.mean(centred * centred, -1, keepdims=True)
    return centred * lax.rsqrt(var + EPS) * gain


def gelu(x):
    return 0.5 * x * (1.0 + lax.erf(x * 0.7071067811865476))


def attend(q, k, v, extra, mask, lane_head, hd):
    per, lanes = q.shape
    lhs = jnp.concatenate([jnp.where(lane_head == j, q, 0.0) for j in range(GROUP)], 0).astype(BF16)
    sc = lax.dot_general(lhs, k, (((1,), (1,)), ((), ())), preferred_element_type=F32)
    sc = sc + extra.reshape(GROUP * per, KEYS) + mask
    top = jnp.max(sc, -1, keepdims=True)
    p = jnp.exp2(sc - top).astype(BF16)
    v = jnp.concatenate([v, jnp.ones(v.shape, BF16)], 1)
    o = jnp.dot(p, v, preferred_element_type=F32)
    num, den = o[:per, :lanes], o[:per, lanes:]
    for j in range(1, GROUP):
        here = lane_head == j
        num = jnp.where(here, o[j * per : (j + 1) * per, :lanes], num)
        den = jnp.where(here, o[j * per : (j + 1) * per, lanes:], den)
    return num / den


def project(blocks, w_qkv, q_scr, k_scr, v_scr, scale):
    d = w_qkv.shape[0]
    step = 256
    asking = jnp.concatenate([own[q_lo : q_lo + n, :] for own, _, _, _, _, q_lo, n in blocks], 0)
    rows = jnp.concatenate([ref[...] for own, halo, *_ in blocks for ref in (own, halo)], 0)
    for c in range(0, d, step):
        q = jnp.dot(asking, w_qkv[:, c : c + step], preferred_element_type=F32)
        q_scr[:, c : c + step] = q * scale
        for part, scr in ((d, k_scr), (2 * d, v_scr)):
            y = jnp.dot(rows, w_qkv[:, part + c : part + c + step], preferred_element_type=F32)
            at = 0
            wi = 0
            for own, halo, *_ in blocks:
                size = own.shape[0]
                for i in range(size // HALF):
                    a = y[at + i * HALF : at + (i + 1) * HALF]
                    b = y[at + size + i * HALF : at + size + (i + 1) * HALF]
                    scr[wi, :, c : c + step] = jnp.concatenate([a, b], 0).astype(BF16)
                    wi += 1
                at += 2 * size


def layer_body(blocks, weights, scratch):
    w_qkv, w_proj, w_in, w_out, gain_attn, gain_mlp = weights
    q_scr, k_scr, v_scr, o_scr, mid_scr, acc_scr = scratch
    d = w_proj.shape[0]
    heads = blocks[0][2].shape[0]
    hd = d // heads
    lanes = GROUP * hd
    groups = heads // GROUP
    scale = LOG2E / hd**0.5
    if w_qkv is not None:
        project(blocks, w_qkv, q_scr, k_scr, v_scr, scale)
    base = 0
    wi = 0
    for own, halo, bias, mask_ref, mask_at, q_lo, q_rows in blocks:
        wins = own.shape[0] // HALF
        per = q_rows // wins
        lane_head = lax.broadcasted_iota(jnp.int32, (per, lanes), 1) // hd
        for i in range(wins):
            first = q_lo + i * per - i * HALF
            at = base + i * per
            mask = jnp.concatenate([mask_ref[mask_at + i, first : first + per, :]] * GROUP, 0)
            for g in range(groups):
                o_scr[at : at + per, g * lanes : (g + 1) * lanes] = attend(
                    q_scr[at : at + per, g * lanes : (g + 1) * lanes],
                    k_scr[wi + i, :, g * lanes : (g + 1) * lanes],
                    v_scr[wi + i, :, g * lanes : (g + 1) * lanes],
                    bias[g * GROUP : (g + 1) * GROUP, first : first + per, :],
                    mask,
                    lane_head,
                    hd,
                )
        base += q_rows
        wi += wins
    proj = jnp.dot(o_scr[...].astype(BF16), w_proj[...], preferred_element_type=F32)
    branch = norm_rows(proj, gain_attn[...]).astype(BF16).astype(F32)
    base = 0
    for own, _, _, _, _, q_lo, q_rows in blocks:
        mid_scr[base : base + q_rows, :] = (
            own[q_lo : q_lo + q_rows, :].astype(F32) + branch[base : base + q_rows]
        ).astype(BF16)
        base += q_rows
    ff = w_in.shape[1]
    chunk = FF_CHUNK
    for c in range(0, ff, chunk):
        up = jnp.dot(mid_scr[...], w_in[:, c : c + chunk], preferred_element_type=F32)
        hid = gelu(up).astype(BF16)
        down = jnp.dot(hid, w_out[c : c + chunk, :], preferred_element_type=F32)
        if c == 0:
            acc_scr[...] = down
        else:
            acc_scr[...] += down
    return mid_scr[...].astype(F32) + norm_rows(acc_scr[...], gain_mlp[...])


def near_kernel(own, q, k, v, bias, mask, *refs):
    weights, out, scratch = (None, *refs[:5]), refs[5], (q, k, v, *refs[6:])
    rows, d = own.shape
    res = layer_body([(own, own, bias, mask, 0, 0, rows)], weights, scratch)
    out[...] = res.astype(BF16).reshape(out.shape)


def last_kernel(
    par_ref, near_res, far, far_halo, e_near, e_near_halo, e_far, e_far_halo, *refs
):
    bias_near, bias_far, mask_far, mask_edge = refs[:4]
    weights, out, near_sem, sems, far_buf, edge_buf = refs[4:10], *refs[10:15]
    scratch = refs[15:]
    par = par_ref[0]
    lat = out.shape[0]
    halves = (1 - par, par)
    main = pl.ds(SHIFT_LAT, lat - 2 * SHIFT_LAT)
    first = pltpu.make_async_copy(near_res, out.at[main, halves[0]], near_sem)
    first.start()
    rows = far.shape[0]
    lo, keep = EDGE // 8 * 8, 80
    res = layer_body(
        [
            (far, far_halo, bias_far, mask_far, 0, 0, rows),
            (e_near, e_near_halo, bias_near, mask_edge, 0, lo, keep),
            (e_far, e_far_halo, bias_far, mask_edge, 2, lo, keep),
        ],
        weights,
        scratch,
    )
    far_buf[...] = res[:rows].astype(BF16).reshape(far_buf.shape)
    copies = [pltpu.make_async_copy(far_buf, out.at[main, halves[1]], sems.at[4])]
    copies[0].start()
    shape = edge_buf.shape[2:]
    for side in range(2):
        at = rows + side * keep + EDGE - lo
        for end in range(2):
            part = res[at + end * EDGE : at + (end + 1) * EDGE]
            edge_buf[side, end] = part.reshape(shape).astype(BF16)
            place = pl.ds(end * (lat - SHIFT_LAT), SHIFT_LAT)
            copies.append(
                pltpu.make_async_copy(
                    edge_buf.at[side, end], out.at[place, halves[side]], sems.at[2 * side + end]
                )
            )
            copies[-1].start()
    for copy in copies:
        copy.wait()
    first.wait()


def layer_scratch(total, windows, weights):
    d = weights[1].shape[0]
    return [
        pltpu.VMEM((total, d), F32),
        pltpu.VMEM((windows, KEYS, d), BF16),
        pltpu.VMEM((windows, KEYS, d), BF16),
        pltpu.VMEM((total, d), F32),
        pltpu.VMEM((total, d), BF16),
        pltpu.VMEM((total, d), F32),
    ]


def near_layer(own, qkv, bias, mask, weights):
    rows, d = own.shape
    shape = (rows // ROW, SHIFT_LON, WIN_LEV, d)
    return pl.pallas_call(
        near_kernel,
        in_specs=vmem(11),
        out_specs=vmem(1)[0],
        out_shape=jax.ShapeDtypeStruct(shape, BF16),
        scratch_shapes=layer_scratch(rows, rows // HALF, weights)[3:],
        compiler_params=params(),
        cost_estimate=cost(NEAR_US),
        name="near",
    )(own, *qkv, bias, mask, *weights[1:])


def last_layer(par, near_res, far, far_halo, edges, bias, masks, weights):
    rows, d = far.shape
    lat = rows // ROW + 2 * SHIFT_LAT
    shape = (lat, 2, SHIFT_LON, WIN_LEV, d)
    return pl.pallas_call(
        last_kernel,
        in_specs=[pl.BlockSpec(memory_space=pltpu.SMEM)] + vmem(17),
        out_specs=pl.BlockSpec(memory_space=pl.ANY),
        out_shape=jax.ShapeDtypeStruct(shape, BF16),
        scratch_shapes=[
            pltpu.SemaphoreType.DMA,
            pltpu.SemaphoreType.DMA((5,)),
            pltpu.VMEM((rows // ROW, SHIFT_LON, WIN_LEV, d), BF16),
            pltpu.VMEM((2, 2, SHIFT_LAT, SHIFT_LON, WIN_LEV, d), BF16),
        ]
        + layer_scratch(rows + 160, rows // HALF + 4, weights),
        compiler_params=params(),
        cost_estimate=cost(12),
        name="last",
    )(par, near_res, far, far_halo, *edges, *bias, *masks, *weights)


def per_device(tokens, group_ids, bias_table, w_qkv, w_proj, gain_attn, w_in, w_out, gain_mlp):
    samples, lev, lat_rows, lon_cols, d = tokens.shape
    lon_count = lax.axis_size("lon")
    lat_count = lax.axis_size("lat")
    lon_at = lax.axis_index("lon").astype(jnp.int32)
    lat_at = lax.axis_index("lat").astype(jnp.int32)
    par = lax.rem(lon_at, 2)
    near_pairs = [(i, i ^ 1) for i in range(lon_count)]
    far_pairs = [(i, (i + (1 if i % 2 else -1)) % lon_count) for i in range(lon_count)]
    down_pairs = [(i, (i + 1) % lat_count) for i in range(lat_count)]
    up_pairs = [(i, (i - 1) % lat_count) for i in range(lat_count)]
    at = jnp.stack([par, lat_at, lon_at])
    wins = lat_rows // WIN_LAT + 1

    cells = jnp.transpose(tokens[0], (1, 2, 0, 3)).reshape(lat_rows, 2, SHIFT_LON, lev, d)
    near, far, top, bot = pack(at, cells)
    far_halo = lax.ppermute(far, "lon", far_pairs)
    near_halo = lax.ppermute(near, "lon", near_pairs)
    above = lax.ppermute(bot, "lat", down_pairs)
    below = lax.ppermute(top, "lat", up_pairs)
    bias_near, bias_far, mask_near, mask_far, mask_edge, *qkv = prep(
        at, group_ids, bias_table.T, near, near_halo, w_qkv, wins
    )
    above, below, bias_near = lax.optimization_barrier((above, below, bias_near))
    edge_near, edge_far = edge_pack(above, top, bot, below)
    edge_near_halo = lax.ppermute(edge_near, "lon", near_pairs)
    edge_far_halo = lax.ppermute(edge_far, "lon", far_pairs)
    weights = [w_qkv, w_proj, w_in, w_out, gain_attn.reshape(1, -1), gain_mlp.reshape(1, -1)]
    near, edge_near = lax.optimization_barrier((near, edge_near))
    near_res = near_layer(near, qkv, bias_near, mask_near, weights)
    out = last_layer(
        at,
        near_res,
        far,
        far_halo,
        [edge_near, edge_near_halo, edge_far, edge_far_halo],
        [bias_near, bias_far],
        [mask_far, mask_edge],
        weights,
    )
    return jnp.transpose(out.reshape(lat_rows, lon_cols, lev, d), (2, 0, 1, 3))[None]


def solution(mesh):
    in_specs = (P(None, None, "lat", "lon", None), P(), P(), P(), P(), P(), P(), P(), P())
    out_specs = P(None, None, "lat", "lon", None)
    return jax.shard_map(
        per_device, mesh=mesh, in_specs=in_specs, out_specs=out_specs, check_vma=False
    )
```
